32 devices in a mesh: parts: 2 (over x), pg: 4 (over z), tp: 4 (over y, core).
Axes of the slice: x: 2, y: 2, z: 4, core: 2. Of those that a mesh axis runs over, the one named last changes fastest.
Arguments:
- tokens: bfloat16 [32, 256, 8192], P(('parts', 'pg'), None, 'tp'), parts along dimension 0
- prefix_kv: bfloat16 [32, 512, 1024], P(('parts', 'pg'), None, 'tp'), parts along dimension 0
- counts: int32 [8], P('parts'), parts along dimension 0, may hold values from 0 to 4, as said below
- destinations: int32 [32], P('parts'), parts along dimension 0, may hold values from -1 to 7, as said below
- page_owner: int32 [128], P('parts'), parts along dimension 0, may hold values from 0 to 3, as said below
- prefix_len: int32 [32], P('parts'), parts along dimension 0, may hold values from 0 to 512, as said below
- ln_gain: bfloat16 [8192], replicated, may hold values from 0.099609375 to 1.8984375
- q_weight: bfloat16 [8192, 4096], P(None, 'tp'), may hold values from -0.0625 to 0.0625
- q_bias: bfloat16 [4096], P('tp'), may hold values from -3 to 3
- kv_weight: bfloat16 [8192, 1024], P(None, 'tp'), may hold values from -0.0625 to 0.0625
- kv_bias: bfloat16 [1024], P('tp'), may hold values from -3 to 3
- o_weight: bfloat16 [4096, 8192], P('tp'), may hold values from -0.09375 to 0.09375
Outputs:
- hidden: bfloat16 [16, 256, 8192], P(('parts', 'pg'), None, 'tp'), parts along dimension 0
- kv_pages: bfloat16 [128, 64, 1024], P(('parts', 'pg'), None, 'tp'), parts along dimension 0
The draws below stay inside these ranges and needn't reach their ends.
There are 2 independent parts, one for each index of `parts`. The reference program is written for one: setup_inputs(seed, part) draws one part's arguments, and reference() takes and returns one part's arrays. A program takes and returns all parts, laid end to end along the dimension named above; an argument that names none is the same for every part. Nothing has to cross between parts.
Inputs may be any that keep to these rules, and one draw needn't show every extreme that they name: Group g holds counts[g] spans, in its first source slots; the counts sum to 8; some group holds 4 and some none. `destinations`: every held span names one work slot and every work slot is named by exactly one held span; span j < min(counts[g], 2) of group g names slot g * 2 + j; the other held spans name slots j >= counts[h] of groups h holding fewer than 2; slots holding no span hold -1. `page_owner`: no group owns more than 16 pages of held spans, and some group owns exactly 16; entries of slots holding no span are arbitrary. `prefix_len`: A multiple of 256.
All inputs are finite; a program needn't handle non-finite values.
Results may differ from the reference program's by a relative error of at most 0.0097.
Values may be sent and summed in bfloat16 or wider, within the bound.
No kernel may reach another device: no remote copies, remote signals or barrier semaphores. Data moves between devices by JAX's collectives and lax.ppermute only.
A program may use at most 192 MiB of HBM per device.

```python
import math
import jax
import jax.numpy as jnp
from jax import lax

D = 8192
HQ = 32
KVH = 4
HD = 128
C = 256
PRE = 512
MAXW = 2
PAGE = 64
MAXC = 4
SRC = 16
WORK = 8
PPC = 4
NPAGE = 64
OWNCAP = 16
KVC = 1024
N_PG = 4
N_TP = 4


def balanced_split(key):
    group_order = jax.random.permutation(jax.random.fold_in(key, 11), N_PG)
    shifts = jax.random.randint(jax.random.fold_in(key, 12), (N_PG // 2,), 0, MAXW + 1)
    shifts = shifts.at[0].set(MAXW)
    counts = jnp.zeros((N_PG,), jnp.int32)
    counts = counts.at[group_order[0::2]].set(MAXW + shifts).at[group_order[1::2]].set(MAXW - shifts)
    source_slot = jnp.arange(SRC, dtype=jnp.int32)
    source_group = source_slot // MAXC
    position = source_slot % MAXC
    held = counts[source_group]
    stays_home = position < jnp.minimum(held, MAXW)
    surplus = (position >= MAXW) & (position < held)
    work_slot = jnp.arange(WORK, dtype=jnp.int32)
    empty_slot = work_slot % MAXW >= counts[work_slot // MAXW]
    priority = jax.random.permutation(jax.random.fold_in(key, 13), WORK).astype(jnp.int32)
    empty_first = jnp.argsort(jnp.where(empty_slot, priority, priority + WORK)).astype(jnp.int32)
    surplus_int = surplus.astype(jnp.int32)
    surplus_rank = jnp.cumsum(surplus_int) - surplus_int
    target = empty_first[jnp.clip(surplus_rank, 0, WORK - 1)]
    destinations = jnp.where(stays_home, source_group * MAXW + position, jnp.where(surplus, target, -1))
    return (counts, destinations.astype(jnp.int32), position < held)


def draw_counts(key, part):
    return balanced_split(key)[0]


def draw_destinations(key, part):
    return balanced_split(key)[1]


def draw_page_owner(key, part):
    held_valid = balanced_split(key)[2]
    key = jax.random.fold_in(key, 5)
    per_owner = MAXW * PPC
    group_order = jax.random.permutation(jax.random.fold_in(key, 1), N_PG)
    shifts = jax.random.randint(jax.random.fold_in(key, 2), (N_PG // 2,), 0, per_owner + 1)
    shifts = shifts.at[0].set(per_owner)
    owner_loads = jnp.zeros((N_PG,), jnp.int32)
    owner_loads = owner_loads.at[group_order[0::2]].set(per_owner + shifts).at[group_order[1::2]].set(per_owner - shifts)
    bounds = jnp.cumsum(owner_loads)
    total_pages = N_PG * per_owner
    rank_index = jnp.arange(total_pages, dtype=jnp.int32)
    owner_of_rank = jnp.sum((rank_index[:, None] >= bounds[None, :]).astype(jnp.int32), axis=1)
    shuffled = owner_of_rank[jax.random.permutation(jax.random.fold_in(key, 3), total_pages)]
    page_valid = jnp.repeat(held_valid, PPC).astype(jnp.int32)
    valid_rank = jnp.cumsum(page_valid) - page_valid
    filler = jax.random.randint(jax.random.fold_in(key, 4), (NPAGE,), 0, N_PG)
    return jnp.where(page_valid == 1, shuffled[jnp.clip(valid_rank, 0, total_pages - 1)], filler).astype(jnp.int32)


def draw_prefix_len(key, part):
    key = jax.random.fold_in(key, 7)
    lengths = jax.random.randint(key, (SRC,), 0, PRE // C + 1) * C
    return lengths.at[0].set(PRE).astype(jnp.int32)


def draw_tokens(key, part):
    key = jax.random.fold_in(key, 3)
    row_key, col_key, base_key = jax.random.split(key, 3)
    row_scale = jnp.exp(jax.random.uniform(row_key, (SRC, C, 1), minval=math.log(0.3), maxval=math.log(3.0)))
    base = jax.random.normal(base_key, (SRC, C, D))
    col_scale = jnp.exp(jax.random.uniform(col_key, (1, 1, D), minval=math.log(0.5), maxval=math.log(2.0)))
    return (base * row_scale * col_scale).astype(jnp.bfloat16)


def draw_prefix_kv(key, part):
    key = jax.random.fold_in(key, 4)
    scale_key, base_key = jax.random.split(key, 2)
    shape = (SRC, PRE, 2, KVH, HD)
    column_scale = jnp.exp(jax.random.uniform(scale_key, (1, 1, 1, KVH, HD), minval=math.log(0.5), maxval=math.log(2.0)))
    base = jax.random.normal(base_key, shape)
    return (base * column_scale).reshape(SRC, PRE, KVC).astype(jnp.bfloat16)


def shard_levels(own_key, shape, cuts, smallest, high):
    level, own = 1.0, jax.random.fold_in(own_key, 6)
    for dim, shards_of in cuts:
        draws = jnp.exp(jax.random.uniform(jax.random.fold_in(own, dim), (shards_of,), jnp.float32, smallest / len(cuts), high / len(cuts)))
        level = level * jnp.repeat(draws, shape[dim] // shards_of).reshape([-1 if axis == dim else 1 for axis in range(len(shape))])
    return level


def scatter_about(own_key, extent, deviation, bound, cuts=(), held_as=jnp.bfloat16):
    drawn = jax.random.normal(own_key, extent, jnp.float32) * deviation
    if len(cuts) > 0:
        drawn = shard_levels(own_key, extent, cuts, -0.22, 0.18) * drawn
    return jnp.clip(drawn, min=-bound, max=bound).astype(held_as)


def setup_inputs(seed: int = 0, part: int = 0) -> dict:
    seeds = jax.random.split(jax.random.key(seed), 13)
    part_splits = jax.random.split(jax.random.fold_in(seeds[12], part), 13)
    return {
        "tokens": draw_tokens(jax.random.fold_in(jax.random.fold_in(seeds[12], part), 71), part),
        "prefix_kv": draw_prefix_kv(jax.random.fold_in(jax.random.fold_in(seeds[12], part), 71), part),
        "counts": draw_counts(jax.random.fold_in(jax.random.fold_in(seeds[12], part), 71), part),
        "destinations": draw_destinations(jax.random.fold_in(jax.random.fold_in(seeds[12], part), 71), part),
        "page_owner": draw_page_owner(jax.random.fold_in(jax.random.fold_in(seeds[12], part), 71), part),
        "prefix_len": draw_prefix_len(jax.random.fold_in(jax.random.fold_in(seeds[12], part), 71), part),
        "ln_gain": jnp.clip(1.0 + 0.18 * jax.random.normal(seeds[6], (D,), jnp.float32), 0.099609375, 1.8984375).astype(jnp.bfloat16),
        "q_weight": scatter_about(seeds[7], (D, HQ * HD), D ** -0.5, 0.0625, ((1, 4),)),
        "q_bias": scatter_about(seeds[8], (HQ * HD,), 0.5, 3.0, ((0, 4),)),
        "kv_weight": scatter_about(seeds[9], (D, KVC), D ** -0.5, 0.0625, ((1, 4),)),
        "kv_bias": scatter_about(seeds[10], (KVC,), 0.5, 3.0, ((0, 4),)),
        "o_weight": scatter_about(seeds[11], (HQ * HD, D), (HQ * HD) ** -0.5, 0.09375, ((0, 4),)),
    }


rope_base = 1000000.0
norm_eps = 1e-06

def work_sources(counts, destinations, groups):
    source_count = 2 * MAXW
    source_slot = jnp.arange(groups * source_count, dtype=jnp.int32)
    is_valid = source_slot % source_count < counts[source_slot // source_count]
    work_slot = jnp.arange(groups * MAXW, dtype=jnp.int32)
    matches = is_valid[None, :] & (destinations[None, :] == work_slot[:, None])
    source = lax.optimization_barrier(jnp.sum(jnp.where(matches, source_slot[None, :], 0), axis=1)).astype(jnp.int32)
    filled = jnp.any(matches, axis=1)
    return (source, filled, is_valid)

def page_ranks(is_valid, page_owner, groups):
    pages_per = C // PAGE
    page_valid = jnp.repeat(is_valid, pages_per)
    membership = (page_valid[:, None] & (page_owner[:, None] == jnp.arange(groups, dtype=jnp.int32)[None, :])).astype(jnp.int32)
    earlier_count = jnp.cumsum(membership, axis=0) - membership
    return lax.optimization_barrier(jnp.sum(earlier_count * membership, axis=1)).astype(jnp.int32)

def rope_angles(positions):
    half_dim = HD // 2
    frequency = rope_base ** (-(jnp.arange(half_dim, dtype=jnp.float32) * (2.0 / HD)))
    angles = positions.astype(jnp.float32)[..., None] * frequency
    return (jnp.cos(angles), jnp.sin(angles))

def rotate(vectors, cosine, sine_table):
    half_dim = HD // 2
    first_half = vectors[..., :half_dim]
    second_half = vectors[..., half_dim:]
    return jnp.concatenate([first_half * cosine - second_half * sine_table, second_half * cosine + first_half * sine_table], axis=-1)

def reference(tokens, prefix_kv, counts, destinations, page_owner, prefix_len, ln_gain, q_weight, q_bias, kv_weight, kv_bias, o_weight):
    source, filled, is_valid = work_sources(counts, destinations, N_PG)
    rank_table = page_ranks(is_valid, page_owner, N_PG)
    heads_here = HQ // N_TP
    gain_row = ln_gain.astype(jnp.float32)
    out_rows = o_weight.astype(jnp.float32).reshape(N_TP, heads_here * HD, D)

    def one_span(work_index):
        source_index = source[work_index]
        span_rows = tokens[source_index].astype(jnp.float32)
        prefix_rows = prefix_kv[source_index]
        prefix_start = prefix_len[source_index]
        inv_rms = lax.rsqrt(lax.optimization_barrier(jnp.mean(span_rows * span_rows, axis=-1, keepdims=True)) + norm_eps)
        normed = (span_rows * inv_rms * gain_row).astype(jnp.bfloat16)
        queries = jnp.dot(normed, q_weight, preferred_element_type=jnp.float32) + q_bias.astype(jnp.float32)
        fresh_columns = (jnp.dot(normed, kv_weight, preferred_element_type=jnp.float32) + kv_bias.astype(jnp.float32)).astype(jnp.bfloat16)
        positions = prefix_start + jnp.arange(C, dtype=jnp.int32)
        cosine, sine_table = rope_angles(positions)
        cosine = cosine[:, None, :]
        sine_table = sine_table[:, None, :]
        queries = (rotate(queries.reshape(C, HQ, HD), cosine, sine_table) * HD ** (-0.5)).astype(jnp.bfloat16)
        fresh_columns = fresh_columns.reshape(C, 2, KVH, HD)
        new_keys = rotate(fresh_columns[:, 0].astype(jnp.float32), cosine, sine_table).astype(jnp.bfloat16)
        new_kv = jnp.stack([new_keys, fresh_columns[:, 1]], axis=1)
        all_rows = jnp.concatenate([prefix_rows.reshape(PRE, 2, KVH, HD), new_kv], axis=0).astype(jnp.float32)
        key_rows = all_rows[:, 0]
        value_rows = all_rows[:, 1]
        grouped = queries.astype(jnp.float32).reshape(C, KVH, HQ // KVH, HD)
        scores = jnp.einsum('cngd,lnd->ngcl', grouped, key_rows)
        key_index = jnp.arange(PRE + C, dtype=jnp.int32)
        query_row = jnp.arange(C, dtype=jnp.int32)
        allowed = jnp.where(key_index[None, :] < PRE, key_index[None, :] < prefix_start, key_index[None, :] - PRE <= query_row[:, None])
        scores = jnp.where(allowed, scores, -jnp.inf)
        row_max = lax.optimization_barrier(jnp.max(scores, axis=-1, keepdims=True))
        weights = jnp.exp(scores - row_max)
        probabilities = (weights / lax.optimization_barrier(jnp.sum(weights, axis=-1, keepdims=True))).astype(jnp.bfloat16)
        mixed_heads = jnp.einsum('ngcl,lnd->cngd', probabilities.astype(jnp.float32), value_rows).astype(jnp.bfloat16)
        heads_out = mixed_heads.reshape(C, N_TP, heads_here * HD).astype(jnp.float32)
        head_term = jnp.einsum('cti,tid->tcd', heads_out, out_rows).astype(jnp.bfloat16)
        head_term = lax.optimization_barrier(head_term).astype(jnp.float32)
        hidden_rows = (span_rows + lax.optimization_barrier(jnp.sum(head_term, axis=0))).astype(jnp.bfloat16)
        hidden_rows = jnp.where(filled[work_index], hidden_rows, jnp.zeros_like(hidden_rows))
        return (hidden_rows, new_kv.reshape(C, KVC))
    hidden, new_all = lax.map(one_span, jnp.arange(WORK, dtype=jnp.int32))
    pages_per = C // PAGE
    page_rows = new_all.reshape(WORK * pages_per, PAGE, KVC)
    work_page = jnp.arange(WORK * pages_per, dtype=jnp.int32)
    source_page = source[work_page // pages_per] * pages_per + work_page % pages_per
    placeable = filled[work_page // pages_per] & (rank_table[source_page] < OWNCAP)
    target = jnp.where(placeable, page_owner[source_page] * OWNCAP + rank_table[source_page], N_PG * OWNCAP).astype(jnp.int32)
    kv_pages = jnp.zeros((N_PG * OWNCAP, PAGE, KVC), jnp.bfloat16).at[target].set(page_rows, mode='drop')
    return (hidden, kv_pages)
```

```python
import functools
import itertools

import jax
import jax.numpy as jnp
from jax import lax
from jax.experimental import pallas as pl
from jax.experimental.pallas import tpu as pltpu
from jax.sharding import PartitionSpec as P

D = 8192
HQ = 32
KVH = 4
HD = 128
C = 256
PRE = 512
MAXW = 2
PAGE = 64
OWNCAP = 16


rope_base = 1000000.0
norm_eps = 1e-06


def work_sources(counts, destinations, groups):
    source_count = 2 * MAXW
    source_slot = jnp.arange(groups * source_count, dtype=jnp.int32)
    is_valid = source_slot % source_count < counts[source_slot // source_count]
    work_slot = jnp.arange(groups * MAXW, dtype=jnp.int32)
    matches = is_valid[None, :] & (destinations[None, :] == work_slot[:, None])
    source = jnp.sum(jnp.where(matches, source_slot[None, :], 0), axis=1)
    filled = jnp.any(matches, axis=1)
    return (source, filled, is_valid)


def page_ranks(is_valid, page_owner, groups):
    pages_per = C // PAGE
    page_valid = jnp.repeat(is_valid, pages_per)
    membership = (
        page_valid[:, None] & (page_owner[:, None] == jnp.arange(groups, dtype=jnp.int32)[None, :])
    ).astype(jnp.int32)
    earlier_count = jnp.cumsum(membership, axis=0) - membership
    return jnp.sum(earlier_count * membership, axis=1)


def rope_angles(positions):
    half_dim = HD // 2
    frequency = rope_base ** (-(jnp.arange(half_dim, dtype=jnp.float32) * (2.0 / HD)))
    angles = positions.astype(jnp.float32)[..., None] * frequency
    return (jnp.cos(angles), jnp.sin(angles))


def rotate(vectors, cosine, sine_table):
    half_dim = HD // 2
    first_half = vectors[..., :half_dim]
    second_half = vectors[..., half_dim:]
    return jnp.concatenate(
        [
            first_half * cosine - second_half * sine_table,
            second_half * cosine + first_half * sine_table,
        ],
        axis=-1,
    )


def head_block(rows, first_head, head_count):
    key_part = lax.dynamic_slice_in_dim(rows, first_head * HD, head_count * HD, 2)
    value_part = lax.dynamic_slice_in_dim(rows, KVH * HD + first_head * HD, head_count * HD, 2)
    return jnp.concatenate([key_part, value_part], axis=2)


GROUPS = 4
SHARD = D // KVH
HEADS = HQ // KVH
SLICE = 2 * HD
VMEM_LIMIT = 40 * 1024 * 1024
GROUP_PAIRS = [(a, b) for a in range(GROUPS) for b in range(GROUPS) if a != b]


def round_patterns():
    double = []
    for senders in itertools.combinations(range(GROUPS), 2):
        low, high = [g for g in range(GROUPS) if g not in senders]
        double.append([(senders[0], low), (senders[1], high)])
        double.append([(senders[0], high), (senders[1], low)])
    return [[pair] for pair in GROUP_PAIRS] + double


def leave_copies(slot, tokens_ref, prefix_ref, leave_ref, sems):
    return [
        pltpu.make_async_copy(tokens_ref.at[slot], leave_ref.at[:, pl.ds(0, SHARD)], sems.at[0])
    ] + [
        pltpu.make_async_copy(
            prefix_ref.at[slot, pl.ds(half * C, C)],
            leave_ref.at[:, pl.ds(SHARD + half * SLICE, SLICE)],
            sems.at[1 + half],
        )
        for half in range(2)
    ]


def route_kernel(
    group_ref, counts_ref, destinations_ref, prefix_len_ref, tokens_ref, prefix_ref,
    out_ref, first_ref, second_ref, leave_first, leave_second, sems,
):
    group = group_ref[0]
    counts = [counts_ref[g] for g in range(GROUPS)]

    def pick(flags, default):
        found = jnp.int32(default)
        for g in reversed(range(GROUPS)):
            found = jnp.where(flags[g], g, found)
        return found

    full = pick([count == 2 * MAXW for count in counts], 0)
    other = pick([(counts[g] > MAXW) & (full != g) for g in range(GROUPS)], -1)
    other_group = jnp.maximum(other, 0)
    other_spare = jnp.where(other >= 0, counts_ref[other_group] - MAXW, 0)
    full_to = [destinations_ref[full * 4 + 2 + i] for i in range(2)]
    other_to = [destinations_ref[other_group * 4 + 2 + i] for i in range(2)]
    clash_first = (other_spare > 0) & (full_to[0] // MAXW == other_to[0] // MAXW)
    clash_second = (other_spare > 1) & (full_to[1] // MAXW == other_to[1] // MAXW)
    swapped = clash_first | clash_second
    got, slots, origins, copies = [], [], [], []
    for r in range(2):
        a, b = full, full_to[r] // MAXW
        take = jnp.where(swapped, 1 - r, r)
        second = other_spare > take
        to = jnp.where(swapped, other_to[1 - r], other_to[r])
        c, d = other_group, to // MAXW
        single_index = a * 3 + b - (b > a).astype(jnp.int32)
        low, high = jnp.minimum(a, c), jnp.maximum(a, c)
        low_to = jnp.where(a < c, b, d)
        high_to = jnp.where(a < c, d, b)
        pair = jnp.where(low == 0, 0, jnp.where(low == 1, 3, 5)) + high - low - 1
        double_index = 12 + 2 * pair + (low_to > high_to).astype(jnp.int32)
        (first_ref, second_ref)[r][0] = jnp.where(second, double_index, single_index)
        leaving = jnp.where((group == c) & second, 2 + take, 2 + r)
        leave_ref = (leave_first, leave_second)[r]
        copies += leave_copies(leaving, tokens_ref, prefix_ref, leave_ref, sems.at[r])
        for copy in copies[-3:]:
            copy.start()
        from_full = b == group
        from_other = second & (d == group)
        got.append(from_full | from_other)
        slots.append(jnp.where(from_full, full_to[r], to) % MAXW)
        origins.append(jnp.where(from_full, a * 4 + 2 + r, c * 4 + 2 + take))
    for r in range(2):
        home_slot = jnp.where(got[1 - r], 1 - slots[1 - r], r)
        slot = jnp.where(got[r], slots[r], home_slot)
        origin = jnp.where(got[r], origins[r], group * 4 + slot)
        out_ref[4 + r] = jnp.where(got[r], 0, 1)
        out_ref[6 + r] = slot
        out_ref[8 + r] = prefix_len_ref[origin]
    for copy in copies:
        copy.wait()


def route(group, counts, destinations, prefix_len, tokens, prefix_kv):
    smem = pl.BlockSpec(memory_space=pltpu.SMEM)
    anywhere = pl.BlockSpec(memory_space=pl.ANY)
    vmem = pl.BlockSpec(memory_space=pltpu.VMEM)
    leaving = jax.ShapeDtypeStruct((C, SHARD + 2 * SLICE), jnp.bfloat16)
    one = jax.ShapeDtypeStruct((1,), jnp.int32)
    return pl.pallas_call(
        route_kernel,
        out_shape=(jax.ShapeDtypeStruct((16,), jnp.int32), one, one, leaving, leaving),
        in_specs=[smem] * 4 + [anywhere] * 2,
        out_specs=(smem, smem, smem, vmem, vmem),
        scratch_shapes=[pltpu.SemaphoreType.DMA((2, 3))],
        name="route",
    )(group.reshape(1), counts, destinations, prefix_len, tokens, prefix_kv)


def settle_kernel(
    r, plan_ref, tokens_ref, prefix_ref, arrived_ref, rows_ref, old_ref, sems
):
    at_home = plan_ref[4 + r] == 1
    slot = plan_ref[6 + r]

    @pl.when(at_home)
    def _():
        pltpu.make_async_copy(tokens_ref.at[slot], rows_ref, sems.at[0]).start()
        for half in range(2):
            here = pl.ds(half * C, C)
            pltpu.make_async_copy(
                prefix_ref.at[slot, here], old_ref.at[here], sems.at[1 + half]
            ).start()

    moved = [
        pltpu.make_async_copy(arrived_ref.at[:, pl.ds(0, SHARD)], rows_ref, sems.at[0])
    ] + [
        pltpu.make_async_copy(
            arrived_ref.at[:, pl.ds(SHARD + half * SLICE, SLICE)],
            old_ref.at[pl.ds(half * C, C)],
            sems.at[1 + half],
        )
        for half in range(2)
    ]

    @pl.when(jnp.logical_not(at_home))
    def _():
        for copy in moved:
            copy.start()

    for copy in moved:
        copy.wait()


def settle(r, plan, tokens, prefix_kv, arrived):
    anywhere = pl.BlockSpec(memory_space=pl.ANY)
    vmem = pl.BlockSpec(memory_space=pltpu.VMEM)
    return pl.pallas_call(
        functools.partial(settle_kernel, r),
        out_shape=(
            jax.ShapeDtypeStruct((C, SHARD), jnp.bfloat16),
            jax.ShapeDtypeStruct((PRE, SLICE), jnp.bfloat16),
        ),
        in_specs=[pl.BlockSpec(memory_space=pltpu.SMEM)] + [anywhere] * 3,
        out_specs=(vmem, vmem),
        scratch_shapes=[pltpu.SemaphoreType.DMA((3,))],
        name=f"settle_{r}",
    )(plan, tokens, prefix_kv, arrived)


def turn(block, cosine, sine):
    return block * cosine + pltpu.roll(block, HD // 2, 1) * sine


def fresh_kernel(
    column_ref, x0, x1, x2, x3, gain_ref, weight_ref, bias_ref, cos_ref, sin_ref,
    normed_ref, fresh_ref, held_ref, sems,
):
    column = column_ref[0]
    copies = [
        pltpu.make_async_copy(weight_ref.at[k], held_ref.at[k], sems.at[k]) for k in range(KVH)
    ]
    for copy in copies:
        copy.start()
    pieces = (x0, x1, x2, x3)

    def rows(i, carry):
        here = pl.ds(pl.multiple_of(i * 16, 16), 16)
        total = jnp.zeros((16, 1), jnp.float32)
        for piece in pieces:
            x = piece[here, :].astype(jnp.float32)
            total += jnp.sum(x * x, axis=1, keepdims=True)
        inv_rms = lax.rsqrt(total * (1.0 / D) + norm_eps)
        for k, piece in enumerate(pieces):
            owner = column ^ k
            x = piece[here, :].astype(jnp.float32)
            normed_ref[owner, here, :] = (x * inv_rms * gain_ref[owner]).astype(jnp.bfloat16)
        return carry

    lax.fori_loop(0, C // 16, rows, 0)
    total = jnp.zeros((C, 2 * HD), jnp.float32)
    for k in range(KVH):
        copies[k].wait()
        total += jnp.dot(normed_ref[k], held_ref[k], preferred_element_type=jnp.float32)
    fresh = (total + bias_ref[...].astype(jnp.float32)).astype(jnp.bfloat16)
    is_key = column < KVH // 2
    for h in range(2):
        block = fresh[:, h * HD : (h + 1) * HD]
        turned = turn(block.astype(jnp.float32), cos_ref[...], sin_ref[...]).astype(jnp.bfloat16)
        fresh_ref[:, h * HD : (h + 1) * HD] = jnp.where(is_key, turned, block)


def fresh_rows(column, pieces, gain, kv_weight, kv_bias, cosine, sine):
    vmem = pl.BlockSpec(memory_space=pltpu.VMEM)
    return pl.pallas_call(
        fresh_kernel,
        out_shape=(
            jax.ShapeDtypeStruct((KVH, C, SHARD), jnp.bfloat16),
            jax.ShapeDtypeStruct((C, 2 * HD), jnp.bfloat16),
        ),
        in_specs=[pl.BlockSpec(memory_space=pltpu.SMEM)]
        + [vmem] * 5
        + [pl.BlockSpec(memory_space=pl.ANY)]
        + [vmem] * 3,
        out_specs=(vmem, vmem),
        scratch_shapes=[
            pltpu.VMEM((KVH, SHARD, 2 * HD), jnp.bfloat16),
            pltpu.SemaphoreType.DMA((KVH,)),
        ],
        compiler_params=pltpu.CompilerParams(vmem_limit_bytes=VMEM_LIMIT),
        cost_estimate=pl.CostEstimate(
            flops=2 * C * D * 2 * HD, bytes_accessed=12 * 2**20, transcendentals=0
        ),
        name="fresh",
    )(column, *pieces, gain, kv_weight, kv_bias, cosine, sine)


def query_kernel(normed_ref, weight_ref, bias_ref, cos_ref, sin_ref, out_ref):
    total = jnp.zeros(out_ref.shape, jnp.float32)
    for k in range(KVH):
        total += jnp.dot(normed_ref[k], weight_ref[k], preferred_element_type=jnp.float32)
    total += bias_ref[...].astype(jnp.float32)
    for h in range(out_ref.shape[1] // HD):
        block = turn(total[:, h * HD : (h + 1) * HD], cos_ref[...], sin_ref[...])
        out_ref[:, h * HD : (h + 1) * HD] = (block * HD ** (-0.5)).astype(jnp.bfloat16)


def query_rows(normed, q_weight, q_bias, cosine, sine):
    width = 256
    columns = HEADS * HD
    return pl.pallas_call(
        query_kernel,
        out_shape=jax.ShapeDtypeStruct((C, columns), jnp.bfloat16),
        grid=(columns // width,),
        in_specs=[
            pl.BlockSpec((KVH, C, SHARD), lambda j: (0, 0, 0)),
            pl.BlockSpec((KVH, SHARD, width), lambda j: (0, 0, j)),
            pl.BlockSpec((1, width), lambda j: (0, j)),
            pl.BlockSpec((C, HD), lambda j: (0, 0)),
            pl.BlockSpec((C, HD), lambda j: (0, 0)),
        ],
        out_specs=pl.BlockSpec((C, width), lambda j: (0, j)),
        compiler_params=pltpu.CompilerParams(vmem_limit_bytes=VMEM_LIMIT),
        cost_estimate=pl.CostEstimate(
            flops=2 * C * D * columns, bytes_accessed=20 * 2**20, transcendentals=0
        ),
        name="queries",
    )(normed, q_weight, q_bias, cosine, sine)


def attend_kernel(length_ref, query_ref, old_key, old_value, new_key, new_value, out_ref):
    contract = (((1,), (1,)), ((), ()))
    query = query_ref[...]
    old = lax.dot_general(query, old_key[...], contract, preferred_element_type=jnp.float32)
    new = lax.dot_general(query, new_key[...], contract, preferred_element_type=jnp.float32)
    old_seen = lax.broadcasted_iota(jnp.int32, old.shape, 1) < length_ref[0]
    new_seen = lax.broadcasted_iota(jnp.int32, new.shape, 1) <= lax.broadcasted_iota(
        jnp.int32, new.shape, 0
    )
    old = jnp.where(old_seen, old, -jnp.inf)
    new = jnp.where(new_seen, new, -jnp.inf)
    top = jnp.maximum(
        jnp.max(old, axis=1, keepdims=True), jnp.max(new, axis=1, keepdims=True)
    )
    old = jnp.exp(old - top)
    new = jnp.exp(new - top)
    share = 1.0 / (jnp.sum(old, axis=1, keepdims=True) + jnp.sum(new, axis=1, keepdims=True))
    old = (old * share).astype(jnp.bfloat16)
    new = (new * share).astype(jnp.bfloat16)
    mixed = jnp.dot(old, old_value[...], preferred_element_type=jnp.float32)
    mixed += jnp.dot(new, new_value[...], preferred_element_type=jnp.float32)
    out_ref[...] = mixed.astype(jnp.bfloat16)


def attend(length, queries, old_key, old_value, new_key, new_value):
    whole = lambda rows: pl.BlockSpec((rows, HD), lambda h: (0, 0))
    return pl.pallas_call(
        attend_kernel,
        out_shape=jax.ShapeDtypeStruct((C, HEADS * HD), jnp.bfloat16),
        grid=(HEADS,),
        in_specs=[
            pl.BlockSpec(memory_space=pltpu.SMEM),
            pl.BlockSpec((C, HD), lambda h: (0, h)),
            whole(PRE),
            whole(PRE),
            whole(C),
            whole(C),
        ],
        out_specs=pl.BlockSpec((C, HD), lambda h: (0, h)),
        compiler_params=pltpu.CompilerParams(vmem_limit_bytes=VMEM_LIMIT),
        cost_estimate=pl.CostEstimate(
            flops=4 * C * (PRE + C) * HD * HEADS,
            bytes_accessed=2 * 2**20,
            transcendentals=C * (PRE + C) * HEADS,
        ),
        name="attend",
    )(length, queries, old_key, old_value, new_key, new_value)


def output_kernel(column_ref, heads_ref, weight_ref, *refs):
    out_ref = refs[-1]
    total = jnp.dot(heads_ref[...], weight_ref[...], preferred_element_type=jnp.float32)
    for ref in refs[:-1]:
        total += ref[...].astype(jnp.float32)
    out_ref[...] = total.astype(out_ref.dtype)


def output_block(column, heads, o_weight, step, addends, dtype):
    width = 1024
    blocks = SHARD // width
    local = pl.BlockSpec((C, width), lambda j, column: (0, j))
    return pl.pallas_call(
        output_kernel,
        out_shape=jax.ShapeDtypeStruct((C, SHARD), dtype),
        grid_spec=pltpu.PrefetchScalarGridSpec(
            num_scalar_prefetch=1,
            grid=(blocks,),
            in_specs=[
                pl.BlockSpec((C, HEADS * HD), lambda j, column: (0, 0)),
                pl.BlockSpec(
                    (HEADS * HD, width), lambda j, column: (0, (column[0] ^ step) * blocks + j)
                ),
            ]
            + [local] * len(addends),
            out_specs=local,
        ),
        compiler_params=pltpu.CompilerParams(vmem_limit_bytes=VMEM_LIMIT),
        cost_estimate=pl.CostEstimate(
            flops=2 * C * HEADS * HD * SHARD, bytes_accessed=6 * 2**20, transcendentals=0
        ),
        name=f"output_{step}",
    )(column, heads, o_weight, *addends)


def routed_layer(
    tokens,
    prefix_kv,
    counts,
    destinations,
    page_owner,
    prefix_len,
    ln_gain,
    q_weight,
    q_bias,
    kv_weight,
    kv_bias,
    o_weight,
):
    group_index = lax.axis_index("pg")
    column = lax.axis_index("tp")
    columns = column.reshape(1)
    plan, *choices, leave_first, leave_second = route(
        group_index, counts, destinations, prefix_len, tokens, prefix_kv
    )

    def swap(rows, step):
        return lax.ppermute(rows, "tp", [(i, i ^ step) for i in range(KVH)])

    def spread(rows):
        across = swap(rows, 2)
        return swap(rows, 1), across, swap(across, 1)

    def first_round(pairs, leaving):
        return lax.ppermute(leaving, "pg", pairs)

    def second_round(pairs, leaving, rows):
        return lax.ppermute(leaving, "pg", pairs), spread(rows)

    patterns = round_patterns()

    def own_heads(rows):
        odd = column % 2 == 1
        low, high = rows[..., :HD], rows[..., HD:]
        mine = jnp.where(odd, high, low)
        passed = swap(jnp.where(odd, low, high), 1)
        keeps_own = (column == 0) | (column == KVH - 1)
        kept = jnp.where(keeps_own, mine, passed)
        crossed = swap(jnp.where(keeps_own, passed, mine), 2)
        upper = column >= KVH // 2
        return jnp.where(upper, crossed, kept), jnp.where(upper, kept, crossed)

    lengths = plan[8:10]
    positions = lengths[:, None] + jnp.arange(C, dtype=jnp.int32)[None, :]
    cosine, sine = rope_angles(positions)
    cosine = jnp.concatenate([cosine, cosine], axis=-1)
    sine = jnp.concatenate([-sine, sine], axis=-1)
    gain = ln_gain.astype(jnp.float32).reshape(KVH, 1, SHARD)
    q_blocks = q_weight.reshape(KVH, SHARD, HEADS * HD)
    kv_blocks = kv_weight.reshape(KVH, SHARD, 2 * HD)
    q_row, kv_row = q_bias.reshape(1, -1), kv_bias.reshape(1, -1)

    arrived = lax.switch(
        choices[0][0], [functools.partial(first_round, pairs) for pairs in patterns], leave_first
    )
    settled = [settle(0, plan, tokens, prefix_kv, arrived)]
    arrived, others = lax.switch(
        choices[1][0],
        [functools.partial(second_round, pairs) for pairs in patterns],
        leave_second,
        settled[0][0],
    )
    settled.append(settle(1, plan, tokens, prefix_kv, arrived))
    others, settled[1] = lax.optimization_barrier((others, settled[1]))
    pieces = [(settled[0][0], *others), (settled[1][0], *spread(settled[1][0]))]
    old_keys, old_values = own_heads(jnp.stack([settled[r][1] for r in range(2)]))
    finished, fresh_all = [], []
    for r in range(2):
        normed, fresh = fresh_rows(
            columns, pieces[r], gain, kv_blocks, kv_row, cosine[r], sine[r]
        )
        fresh_all.append(fresh)
        new_key, new_value = own_heads(fresh)
        queries = query_rows(normed, q_blocks, q_row, cosine[r], sine[r])
        heads = attend(lengths[r : r + 1], queries, old_keys[r], old_values[r], new_key, new_value)
        block = functools.partial(output_block, columns, heads, o_weight)
        for_corner = swap(block(3, (), jnp.bfloat16), 1)
        for_beside = swap(block(1, (), jnp.bfloat16), 1)
        for_across = swap(block(2, (for_corner,), jnp.bfloat16), 2)
        kept = block(0, (for_beside,), jnp.float32)
        finished.append(
            (pieces[r][0].astype(jnp.float32) + kept + for_across.astype(jnp.float32)).astype(jnp.bfloat16)
        )
    first = plan[6] == 0
    hidden = jnp.where(first, jnp.stack(finished), jnp.stack(finished[::-1]))

    source, filled, is_valid = work_sources(counts, destinations, GROUPS)
    rank_table = page_ranks(is_valid, page_owner, GROUPS)
    pages_per = C // PAGE
    in_slots = jnp.where(first, jnp.stack(fresh_all), jnp.stack(fresh_all[::-1]))
    gathered = [in_slots] + [
        lax.ppermute(in_slots, "pg", [(i, (i + step) % GROUPS) for i in range(GROUPS)])
        for step in range(1, GROUPS)
    ]
    page_rows = jnp.concatenate(gathered).reshape(GROUPS * MAXW * pages_per, PAGE, 2 * HD)
    work_page = jnp.arange(GROUPS * MAXW * pages_per, dtype=jnp.int32)
    source_page = source[work_page // pages_per] * pages_per + work_page % pages_per
    retained = filled[work_page // pages_per] & (page_owner[source_page] == group_index)
    slot_matches = retained[None, :] & (
        rank_table[source_page][None, :] == jnp.arange(OWNCAP, dtype=jnp.int32)[:, None]
    )
    slot_pick = jnp.sum(jnp.where(slot_matches, work_page[None, :], 0), axis=1)
    group_pages = MAXW * pages_per
    nearby = (group_index - slot_pick // group_pages) % GROUPS * group_pages
    kv_pages = jnp.where(
        jnp.any(slot_matches, axis=1)[:, None, None],
        page_rows[nearby + slot_pick % group_pages],
        jnp.zeros((), jnp.bfloat16),
    )
    return (hidden, kv_pages)


def gathered_layer(
    tokens,
    prefix_kv,
    counts,
    destinations,
    page_owner,
    prefix_len,
    ln_gain,
    q_weight,
    q_bias,
    kv_weight,
    kv_bias,
    o_weight,
):
    groups = lax.axis_size("pg")
    group_index = lax.axis_index("pg")
    column = lax.axis_index("tp")
    source_count = tokens.shape[0]
    heads_here = q_weight.shape[1] // HD
    group_size = HQ // KVH
    local_kv_heads = max(1, heads_here // group_size)
    first_kv_head = column * heads_here // group_size
    slice_width = prefix_kv.shape[2]
    extra_slots = source_count - MAXW
    source, filled, is_valid = work_sources(counts, destinations, groups)
    rank_table = page_ranks(is_valid, page_owner, groups)
    own_sources = lax.dynamic_slice_in_dim(source, group_index * MAXW, MAXW)
    stays_home = jnp.arange(MAXW, dtype=jnp.int32) < counts[group_index]
    spare_index = jnp.arange(groups * extra_slots, dtype=jnp.int32)
    spare_slot = spare_index // extra_slots * source_count + MAXW + spare_index % extra_slots
    spare_valid = MAXW + spare_index % extra_slots < counts[spare_index // extra_slots]
    wanted = group_index * MAXW + jnp.arange(MAXW, dtype=jnp.int32)
    matches = spare_valid[None, :] & (destinations[spare_slot][None, :] == wanted[:, None])
    chosen = jnp.sum(jnp.where(matches, spare_index[None, :], 0), axis=1)

    def settle(own_rows, moved_rows):
        return jnp.where(stays_home[:, None, None], own_rows, moved_rows[chosen])

    gathered = lax.all_gather(prefix_kv, "tp", axis=2, tiled=True)
    head_columns = head_block(gathered, first_kv_head, local_kv_heads)
    moved_tokens, moved_heads = (
        lax.all_gather(tokens[MAXW:], "pg", axis=0, tiled=True),
        lax.all_gather(head_columns[MAXW:], "pg", axis=0, tiled=True),
    )
    work_tokens = settle(tokens[:MAXW], moved_tokens)
    work_prefix = settle(head_columns[:MAXW], moved_heads)
    features = lax.all_gather(work_tokens, "tp", axis=2, tiled=True)
    feature_rows = features.astype(jnp.float32)
    inv_rms = lax.rsqrt(jnp.mean(feature_rows * feature_rows, axis=-1, keepdims=True) + norm_eps)
    normed = (feature_rows * inv_rms * ln_gain.astype(jnp.float32)).astype(jnp.bfloat16)
    flat_normed = normed.reshape(MAXW * C, D)
    queries = jnp.dot(flat_normed, q_weight, preferred_element_type=jnp.float32) + q_bias.astype(
        jnp.float32
    )
    fresh_columns = (
        jnp.dot(flat_normed, kv_weight, preferred_element_type=jnp.float32)
        + kv_bias.astype(jnp.float32)
    ).astype(jnp.bfloat16)
    fresh_all = lax.all_gather(
        fresh_columns.reshape(MAXW, C, slice_width), "tp", axis=2, tiled=True
    )
    prefix_start = prefix_len[own_sources]
    positions = prefix_start[:, None] + jnp.arange(C, dtype=jnp.int32)[None, :]
    cosine, sine_table = rope_angles(positions)
    cosine = cosine[:, :, None, :]
    sine_table = sine_table[:, :, None, :]
    queries = (
        rotate(queries.reshape(MAXW, C, heads_here, HD), cosine, sine_table) * HD ** (-0.5)
    ).astype(jnp.bfloat16)
    fresh_all = fresh_all.reshape(MAXW, C, 2, KVH, HD)
    new_keys = rotate(fresh_all[:, :, 0].astype(jnp.float32), cosine, sine_table).astype(
        jnp.bfloat16
    )
    new_kv = jnp.concatenate(
        [new_keys.reshape(MAXW, C, KVH * HD), fresh_all[:, :, 1].reshape(MAXW, C, KVH * HD)], axis=2
    )
    new_heads = head_block(new_kv, first_kv_head, local_kv_heads)
    all_rows = jnp.concatenate([work_prefix, new_heads], axis=1).reshape(
        MAXW, PRE + C, 2, local_kv_heads, HD
    )
    key_rows = all_rows[:, :, 0]
    value_rows = all_rows[:, :, 1]
    grouped = queries.reshape(MAXW, C, local_kv_heads, heads_here // local_kv_heads, HD)
    scores = jnp.einsum("wcngd,wlnd->wngcl", grouped, key_rows, preferred_element_type=jnp.float32)
    key_index = jnp.arange(PRE + C, dtype=jnp.int32)
    query_row = jnp.arange(C, dtype=jnp.int32)
    allowed = jnp.where(
        key_index[None, None, :] < PRE,
        key_index[None, None, :] < prefix_start[:, None, None],
        (key_index - PRE)[None, None, :] <= query_row[None, :, None],
    )
    scores = jnp.where(allowed[:, None, None], scores, -jnp.inf)
    row_max = jnp.max(scores, axis=-1, keepdims=True)
    weights = jnp.exp(scores - row_max)
    probabilities = (weights / jnp.sum(weights, axis=-1, keepdims=True)).astype(jnp.bfloat16)
    mixed_heads = jnp.einsum(
        "wngcl,wlnd->wcngd", probabilities, value_rows, preferred_element_type=jnp.float32
    ).astype(jnp.bfloat16)
    head_partial = jnp.dot(
        mixed_heads.reshape(MAXW * C, heads_here * HD), o_weight, preferred_element_type=jnp.float32
    ).reshape(MAXW, C, D)
    attended = lax.psum_scatter(
        head_partial.astype(jnp.bfloat16), "tp", scatter_dimension=2, tiled=True
    ).astype(jnp.float32)
    hidden = (work_tokens.astype(jnp.float32) + attended).astype(jnp.bfloat16)
    pages_per = C // PAGE
    own_columns = lax.dynamic_slice_in_dim(new_kv, column * slice_width, slice_width, 2)
    page_rows = own_columns.reshape(MAXW * pages_per, PAGE, slice_width)
    work_page = jnp.arange(groups * MAXW * pages_per, dtype=jnp.int32)
    source_page = source[work_page // pages_per] * pages_per + work_page % pages_per
    owner_of_page = page_owner[source_page]
    local_owner = lax.dynamic_slice_in_dim(
        owner_of_page, group_index * MAXW * pages_per, MAXW * pages_per
    )
    addressed = local_owner[None, :] == jnp.arange(groups, dtype=jnp.int32)[:, None]
    outbox = jnp.where(addressed[:, :, None, None], page_rows[None], jnp.zeros((), jnp.bfloat16))
    arrived = lax.all_to_all(outbox, "pg", split_axis=0, concat_axis=0, tiled=True).reshape(
        groups * MAXW * pages_per, PAGE, slice_width
    )
    retained = filled[work_page // pages_per] & (owner_of_page == group_index)
    slot_matches = retained[None, :] & (
        rank_table[source_page][None, :] == jnp.arange(OWNCAP, dtype=jnp.int32)[:, None]
    )
    slot_pick = jnp.sum(jnp.where(slot_matches, work_page[None, :], 0), axis=1)
    kv_pages = jnp.where(
        jnp.any(slot_matches, axis=1)[:, None, None],
        arrived[slot_pick],
        jnp.zeros((), jnp.bfloat16),
    )
    return (hidden, kv_pages)


def solution(mesh):
    in_specs = (
        P(("parts", "pg"), None, "tp"),
        P(("parts", "pg"), None, "tp"),
        P("parts"),
        P("parts"),
        P("parts"),
        P("parts"),
        P(),
        P(None, "tp"),
        P("tp"),
        P(None, "tp"),
        P("tp"),
        P("tp", None),
    )
    out_specs = (P(("parts", "pg"), None, "tp"), P(("parts", "pg"), None, "tp"))
    if mesh.shape["pg"] == 4 and mesh.shape["tp"] == KVH:
        layer = routed_layer
    else:
        layer = gathered_layer
    return jax.shard_map(layer, mesh=mesh, in_specs=in_specs, out_specs=out_specs, check_vma=False)
```

```python
import functools
import itertools

import jax
import jax.numpy as jnp
import numpy as np
from jax import lax
from jax.experimental import pallas as pl
from jax.experimental.pallas import tpu as pltpu
from jax.sharding import PartitionSpec as P

D = 8192
HQ = 32
KVH = 4
HD = 128
C = 256
PRE = 512
MAXW = 2
PAGE = 64
OWNCAP = 16


rope_base = 1000000.0
norm_eps = 1e-06


def work_sources(counts, destinations, groups):
    source_count = 2 * MAXW
    source_slot = jnp.arange(groups * source_count, dtype=jnp.int32)
    is_valid = source_slot % source_count < counts[source_slot // source_count]
    work_slot = jnp.arange(groups * MAXW, dtype=jnp.int32)
    matches = is_valid[None, :] & (destinations[None, :] == work_slot[:, None])
    source = jnp.sum(jnp.where(matches, source_slot[None, :], 0), axis=1)
    filled = jnp.any(matches, axis=1)
    return (source, filled, is_valid)


def page_ranks(is_valid, page_owner, groups):
    pages_per = C // PAGE
    page_valid = jnp.repeat(is_valid, pages_per)
    membership = (
        page_valid[:, None] & (page_owner[:, None] == jnp.arange(groups, dtype=jnp.int32)[None, :])
    ).astype(jnp.int32)
    earlier_count = jnp.cumsum(membership, axis=0) - membership
    return jnp.sum(earlier_count * membership, axis=1)


def rope_angles(positions):
    half_dim = HD // 2
    frequency = rope_base ** (-(jnp.arange(half_dim, dtype=jnp.float32) * (2.0 / HD)))
    angles = positions.astype(jnp.float32)[..., None] * frequency
    return (jnp.cos(angles), jnp.sin(angles))


def rotate(vectors, cosine, sine_table):
    half_dim = HD // 2
    first_half = vectors[..., :half_dim]
    second_half = vectors[..., half_dim:]
    return jnp.concatenate(
        [
            first_half * cosine - second_half * sine_table,
            second_half * cosine + first_half * sine_table,
        ],
        axis=-1,
    )


def head_block(rows, first_head, head_count):
    key_part = lax.dynamic_slice_in_dim(rows, first_head * HD, head_count * HD, 2)
    value_part = lax.dynamic_slice_in_dim(rows, KVH * HD + first_head * HD, head_count * HD, 2)
    return jnp.concatenate([key_part, value_part], axis=2)


GROUPS = 4
SHARD = D // KVH
HEADS = HQ // KVH
SLICE = 2 * HD
HALF = C // 2
NORM_ROWS = 16
OUT_PARTS = 2
ADD_PARTS = 4
GROUP_PAIRS = [(a, b) for a in range(GROUPS) for b in range(GROUPS) if a != b]
SMEM = pl.BlockSpec(memory_space=pltpu.SMEM)
VMEM = pl.BlockSpec(memory_space=pltpu.VMEM)
HBM = pl.BlockSpec(memory_space=pltpu.HBM)
ANY = pl.BlockSpec(memory_space=pl.ANY)
QUICK = pl.CostEstimate(flops=1, bytes_accessed=1, transcendentals=0)


def kernel_params(mib):
    return pltpu.CompilerParams(vmem_limit_bytes=mib * 2**20)


def rows_of(*shape, dtype=jnp.bfloat16):
    return jax.ShapeDtypeStruct(shape, dtype)


def start_all(copies):
    for copy in copies:
        copy.start()
    return copies


def rope_tables():
    frequency = rope_base ** (-(np.arange(HD // 2, dtype=np.float32) * np.float32(2.0 / HD)))
    positions = np.arange(PRE + C, dtype=np.float32)
    angles = positions[:, None] * frequency.astype(np.float32)
    cosine, sine = np.cos(angles), np.sin(angles)
    tables = (np.concatenate([cosine, cosine], 1), np.concatenate([-sine, sine], 1))
    return [jnp.asarray(t.astype(np.float32).reshape(-1, C, HD)) for t in tables]


def round_patterns():
    double = []
    for senders in itertools.combinations(range(GROUPS), 2):
        low, high = [g for g in range(GROUPS) if g not in senders]
        double.append([(senders[0], low), (senders[1], high)])
        double.append([(senders[0], high), (senders[1], low)])
    return [[pair] for pair in GROUP_PAIRS] + double


def leave_copies(slot, tokens_ref, prefix_ref, leave_ref, sems):
    return [
        pltpu.make_async_copy(tokens_ref.at[slot], leave_ref.at[:, pl.ds(0, SHARD)], sems.at[0])
    ] + [
        pltpu.make_async_copy(
            prefix_ref.at[slot, pl.ds(half * C, C)],
            leave_ref.at[:, pl.ds(SHARD + half * SLICE, SLICE)],
            sems.at[1 + half],
        )
        for half in range(2)
    ]


def route_kernel(
    group_ref, counts_ref, destinations_ref, prefix_len_ref, tokens_ref, prefix_ref,
    plan_ref, first_ref, second_ref, leave_first, leave_second, table_ref, sems,
):
    group = group_ref[0]
    counts = [counts_ref[g] for g in range(GROUPS)]

    def pick(flags, default):
        found = jnp.int32(default)
        for g in reversed(range(GROUPS)):
            found = jnp.where(flags[g], g, found)
        return found

    full = pick([count == 2 * MAXW for count in counts], 0)
    other = pick([(counts[g] > MAXW) & (full != g) for g in range(GROUPS)], -1)
    other_group = jnp.maximum(other, 0)
    other_spare = jnp.where(other >= 0, counts_ref[other_group] - MAXW, 0)
    full_to = [destinations_ref[full * 4 + 2 + i] for i in range(2)]
    other_to = [destinations_ref[other_group * 4 + 2 + i] for i in range(2)]
    clash_first = (other_spare > 0) & (full_to[0] // MAXW == other_to[0] // MAXW)
    clash_second = (other_spare > 1) & (full_to[1] // MAXW == other_to[1] // MAXW)
    swapped = clash_first | clash_second
    moves, copies = [], []
    for r in range(2):
        a, b = full, full_to[r] // MAXW
        take = jnp.where(swapped, 1 - r, r)
        second = other_spare > take
        to = jnp.where(swapped, other_to[1 - r], other_to[r])
        c, d = other_group, to // MAXW
        single_index = a * 3 + b - (b > a).astype(jnp.int32)
        low, high = jnp.minimum(a, c), jnp.maximum(a, c)
        low_to = jnp.where(a < c, b, d)
        high_to = jnp.where(a < c, d, b)
        pair = jnp.where(low == 0, 0, jnp.where(low == 1, 3, 5)) + high - low - 1
        double_index = 12 + 2 * pair + (low_to > high_to).astype(jnp.int32)
        (first_ref, second_ref)[r][0] = jnp.where(second, double_index, single_index)
        leaving = jnp.where((group == c) & second, 2 + take, 2 + r)
        leave_ref = (leave_first, leave_second)[r]
        copies += start_all(leave_copies(leaving, tokens_ref, prefix_ref, leave_ref, sems.at[r]))
        moves.append((a, b, full_to[r], 2 + r, second, c, d, to, 2 + take))
    for g in range(GROUPS):
        got, slots, origins = [], [], []
        for a, b, a_to, a_slot, second, c, d, c_to, c_slot in moves:
            from_full = b == g
            got.append(from_full | (second & (d == g)))
            slots.append(jnp.where(from_full, a_to, c_to) % MAXW)
            origins.append(jnp.where(from_full, a * 4 + a_slot, c * 4 + c_slot))
        for r in range(2):
            home_slot = jnp.where(got[1 - r], 1 - slots[1 - r], r)
            slot = jnp.where(got[r], slots[r], home_slot)
            table_ref[g * 8 + r] = jnp.where(got[r], 0, 1)
            table_ref[g * 8 + 2 + r] = slot
            table_ref[g * 8 + 4 + r] = prefix_len_ref[jnp.where(got[r], origins[r], g * 4 + slot)]
            if r == 0:
                plan_ref[8 + g] = slot
    for i in range(6):
        plan_ref[i] = table_ref[group * 8 + i]
    for copy in copies:
        copy.wait()


def route(group, counts, destinations, prefix_len, tokens, prefix_kv):
    leaving = rows_of(C, SHARD + 2 * SLICE)
    one = rows_of(1, dtype=jnp.int32)
    return pl.pallas_call(
        route_kernel,
        out_shape=(rows_of(16, dtype=jnp.int32), one, one, leaving, leaving),
        in_specs=[SMEM] * 4 + [ANY] * 2,
        out_specs=(SMEM, SMEM, SMEM, VMEM, VMEM),
        scratch_shapes=[
            pltpu.SMEM((GROUPS * 8,), jnp.int32),
            pltpu.SemaphoreType.DMA((2, 3)),
        ],
        cost_estimate=QUICK,
        name="route",
    )(group, counts, destinations, prefix_len, tokens, prefix_kv)


def settle_kernel(
    r, column_ref, plan_ref, tokens_ref, prefix_ref, arrived_ref, rows_ref, mine_ref, other_ref, *refs
):
    halves_of_rows, sems = refs[:-1], refs[-1]
    at_home = plan_ref[r] == 1
    slot = plan_ref[2 + r]
    odd = column_ref[0] % 2
    halves = [(half, part) for half in range(PRE // C) for part in range(2)]

    def token_copies(source):
        whole = [pltpu.make_async_copy(source, rows_ref, sems.at[0])]
        return whole + [
            pltpu.make_async_copy(source.at[pl.ds(half * HALF, HALF)], ref, sems.at[5 + half])
            for half, ref in enumerate(halves_of_rows)
        ]

    def head(half, part):
        target = (mine_ref, other_ref)[part].at[pl.ds(half * C, C)]
        side = pl.multiple_of(jnp.where(odd == part, 0, HD), HD)
        return target, side

    @pl.when(at_home)
    def _():
        start_all(token_copies(tokens_ref.at[slot]))
        for i, (half, part) in enumerate(halves):
            target, side = head(half, part)
            source = prefix_ref.at[slot, pl.ds(half * C, C), pl.ds(side, HD)]
            pltpu.make_async_copy(source, target, sems.at[1 + i]).start()

    moved = token_copies(arrived_ref.at[:, pl.ds(0, SHARD)])
    for i, (half, part) in enumerate(halves):
        target, side = head(half, part)
        place = pl.multiple_of(SHARD + half * SLICE + side, HD)
        source = arrived_ref.at[:, pl.ds(place, HD)]
        moved.append(pltpu.make_async_copy(source, target, sems.at[1 + i]))

    @pl.when(jnp.logical_not(at_home))
    def _():
        start_all(moved)

    for copy in moved:
        copy.wait()


def settle(r, column, plan, tokens, prefix_kv, arrived):
    return pl.pallas_call(
        functools.partial(settle_kernel, r),
        out_shape=(rows_of(C, SHARD), rows_of(PRE, HD), rows_of(PRE, HD))
        + (rows_of(HALF, SHARD),) * (2 * r),
        in_specs=[SMEM] * 2 + [ANY] * 3,
        out_specs=(VMEM,) * (3 + 2 * r),
        scratch_shapes=[pltpu.SemaphoreType.DMA((3 + 2 * (PRE // C),))],
        cost_estimate=QUICK,
        name=f"settle_{r}",
    )(column, plan, tokens, prefix_kv, arrived)


def turn(block, cosine, sine):
    return block * cosine + pltpu.roll(block, HD // 2, 1) * sine


def table_copies(r, plan_ref, tables, held_ref, sems):
    block = plan_ref[4 + r] // C
    return [
        pltpu.make_async_copy(table.at[block], held_ref.at[i], sems.at[i])
        for i, table in enumerate(tables)
    ]


def fresh_kernel(r, split, column_ref, plan_ref, gain_ref, bias_ref, *refs):
    pieces, refs = refs[: sum(split)], refs[sum(split) :]
    cos_ref, sin_ref, weight_ref, normed_ref, fresh_ref, mine_ref, other_ref = refs[:7]
    held_ref, turn_ref, sems, turn_sems = refs[7:]
    column = column_ref[0]
    copies = start_all(
        [pltpu.make_async_copy(weight_ref.at[k], held_ref.at[k], sems.at[k]) for k in range(KVH)]
    )
    turns = start_all(table_copies(r, plan_ref, (cos_ref, sin_ref), turn_ref, turn_sems))

    for half in range(2):
        sources, at = [], 0
        for parts in split:
            sources.append((pieces[at + half], 0) if parts == 2 else (pieces[at], half * HALF))
            at += parts

        def rows(i, carry):
            start = i * NORM_ROWS
            blocks = [
                (ref, pl.ds(pl.multiple_of(first + start, NORM_ROWS), NORM_ROWS))
                for ref, first in sources
            ]
            total = jnp.zeros((NORM_ROWS, HD), jnp.float32)
            for ref, here in blocks:
                for j in range(SHARD // HD):
                    x = ref[here, j * HD : (j + 1) * HD].astype(jnp.float32)
                    total += x * x
            inv_rms = lax.rsqrt(jnp.sum(total, axis=1, keepdims=True) * (1.0 / D) + norm_eps)
            there = pl.ds(pl.multiple_of(half * HALF + start, NORM_ROWS), NORM_ROWS)
            for k, (ref, here) in enumerate(blocks):
                owner = column ^ k
                x = ref[here, :].astype(jnp.float32)
                normed_ref[owner, there, :] = (x * inv_rms * gain_ref[owner]).astype(jnp.bfloat16)
            return carry

        lax.fori_loop(0, HALF // NORM_ROWS, rows, 0, unroll=4)
    terms = []
    for k in range(KVH):
        copies[k].wait()
        terms.append(jnp.dot(normed_ref[k], held_ref[k], preferred_element_type=jnp.float32))
    total = (terms[0] + terms[1]) + (terms[2] + terms[3])
    fresh = (total + bias_ref[...].astype(jnp.float32)).astype(jnp.bfloat16)
    for copy in turns:
        copy.wait()
    is_key = column < KVH // 2
    blocks = []
    for h in range(2):
        block = fresh[:, h * HD : (h + 1) * HD]
        turned = turn(block.astype(jnp.float32), turn_ref[0], turn_ref[1]).astype(jnp.bfloat16)
        blocks.append(jnp.where(is_key, turned, block))
        fresh_ref[:, h * HD : (h + 1) * HD] = blocks[h]
    odd = column % 2 == 1
    mine_ref[...] = jnp.where(odd, blocks[1], blocks[0])
    other_ref[...] = jnp.where(odd, blocks[0], blocks[1])


def fresh_rows(r, column, plan, pieces, gain, kv_weight, kv_bias, tables):
    flat = [part for piece in pieces for part in piece]
    head = rows_of(C, HD)
    return pl.pallas_call(
        functools.partial(fresh_kernel, r, [len(piece) for piece in pieces]),
        out_shape=(rows_of(KVH, C, SHARD), rows_of(C, SLICE), head, head),
        in_specs=[SMEM] * 2 + [VMEM] * (2 + len(flat)) + [HBM] * 3,
        out_specs=(VMEM,) * 4,
        scratch_shapes=[
            pltpu.VMEM((KVH, SHARD, SLICE), jnp.bfloat16),
            pltpu.VMEM((2, C, HD), jnp.float32),
            pltpu.SemaphoreType.DMA((KVH,)),
            pltpu.SemaphoreType.DMA((2,)),
        ],
        compiler_params=kernel_params(16),
        cost_estimate=QUICK,
        name=f"fresh_{r}",
    )(column, plan, gain, kv_bias, *flat, *tables, kv_weight)


def query_kernel(
    r, plan_ref, normed_ref, bias_ref, cos_ref, sin_ref, weight_ref,
    out_ref, held_ref, total_ref, turn_ref, sems, turn_sems,
):
    depth = SHARD // 2
    start_all(
        [
            pltpu.make_async_copy(
                weight_ref.at[i // 2, pl.ds(i % 2 * depth, depth)], held_ref.at[i], sems.at[i]
            )
            for i in range(2 * KVH)
        ]
    )
    turns = start_all(table_copies(r, plan_ref, (cos_ref, sin_ref), turn_ref, turn_sems))
    total_ref[...] = jnp.broadcast_to(bias_ref[...].astype(jnp.float32), total_ref.shape)

    def add_term(i, carry):
        pltpu.make_async_copy(held_ref.at[i], held_ref.at[i], sems.at[i]).wait()
        here = pl.ds(pl.multiple_of(i % 2 * depth, depth), depth)
        total_ref[...] += jnp.dot(
            normed_ref[i // 2, :, here], held_ref[i], preferred_element_type=jnp.float32
        )
        return carry

    lax.fori_loop(0, 2 * KVH, add_term, 0)
    for copy in turns:
        copy.wait()
    for h in range(HEADS):
        here = slice(h * HD, (h + 1) * HD)
        block = turn(total_ref[:, here], turn_ref[0], turn_ref[1])
        out_ref[:, here] = (block * HD ** (-0.5)).astype(jnp.bfloat16)


def query_rows(r, plan, normed, q_weight, q_bias, tables):
    columns = HEADS * HD
    return pl.pallas_call(
        functools.partial(query_kernel, r),
        out_shape=rows_of(C, columns),
        in_specs=[SMEM] + [VMEM] * 2 + [HBM] * 3,
        out_specs=VMEM,
        scratch_shapes=[
            pltpu.VMEM((2 * KVH, SHARD // 2, columns), jnp.bfloat16),
            pltpu.VMEM((C, columns), jnp.float32),
            pltpu.VMEM((2, C, HD), jnp.float32),
            pltpu.SemaphoreType.DMA((2 * KVH,)),
            pltpu.SemaphoreType.DMA((2,)),
        ],
        compiler_params=kernel_params(24),
        cost_estimate=QUICK,
        name=f"queries_{r}",
    )(plan, normed, q_bias, *tables, q_weight)


def weight_copies(weight_ref, held_ref, block, sems):
    width = SHARD // OUT_PARTS
    return [
        pltpu.make_async_copy(
            weight_ref.at[:, pl.ds(pl.multiple_of(block * SHARD + i * width, width), width)],
            held_ref.at[:, pl.ds(i * width, width)],
            sems.at[i],
        )
        for i in range(OUT_PARTS)
    ]


def multiply_out(rows_ref, held_ref, sems, addends, *outs):
    width = SHARD // OUT_PARTS

    def part(i, carry):
        here = pl.ds(pl.multiple_of(i * width, width), width)
        pltpu.make_async_copy(held_ref.at[:, here], held_ref.at[:, here], sems.at[i]).wait()
        total = jnp.dot(rows_ref[...], held_ref[:, here], preferred_element_type=jnp.float32)
        for ref in addends:
            total += ref[:, here].astype(jnp.float32)
        for k, ref in enumerate(outs):
            height = ref.shape[0]
            ref[:, here] = total[k * height : (k + 1) * height].astype(ref.dtype)
        return carry

    lax.fori_loop(0, OUT_PARTS, part, 0)


def attend_kernel(r, steps, parts, column_ref, plan_ref, query_ref, *refs):
    old_kept, old_crossed, new_kept, new_crossed, weight_ref, heads_ref = refs[:6]
    outs, (held_ref, keys_ref, values_ref, sems) = refs[6:-4], refs[-4:]
    column = column_ref[0]
    for i, step in enumerate(steps):
        start_all(weight_copies(weight_ref, held_ref.at[i], column ^ step, sems.at[i]))
    upper = column >= KVH // 2
    for rows, kept, crossed in ((pl.ds(0, PRE), old_kept, old_crossed), (pl.ds(PRE, C), new_kept, new_crossed)):
        keys_ref[rows, :] = jnp.where(upper, crossed[...], kept[...])
        values_ref[rows, :] = jnp.where(upper, kept[...], crossed[...])
    seen = [
        jnp.where(plan_ref[4 + r] > i * C, 0.0, -jnp.inf).astype(jnp.float32)
        for i in range(PRE // C)
    ]
    causal = lax.broadcasted_iota(jnp.int32, (C, C), 1) <= lax.broadcasted_iota(
        jnp.int32, (C, C), 0
    )
    key_blocks = range(PRE // C + 1)

    def score(h):
        query = query_ref[:, h * HD : (h + 1) * HD]
        scores = lax.dot_general(
            query, keys_ref[...], (((1,), (1,)), ((), ())), preferred_element_type=jnp.float32
        )
        return [scores[:, i * C : (i + 1) * C] for i in key_blocks]

    upcoming = score(0)
    for h in range(HEADS):
        blocks = upcoming
        if h + 1 < HEADS:
            upcoming = score(h + 1)
        blocks = [block + bias for block, bias in zip(blocks, seen)] + [
            jnp.where(causal, blocks[-1], -jnp.inf)
        ]
        top = jnp.max(functools.reduce(jnp.maximum, blocks), axis=1, keepdims=True)
        blocks = [jnp.exp(block - top) for block in blocks]
        share = 1.0 / jnp.sum(functools.reduce(jnp.add, blocks), axis=1, keepdims=True)
        mixed = jnp.zeros((C, HD), jnp.float32)
        for i in key_blocks:
            mixed += jnp.dot(
                blocks[i].astype(jnp.bfloat16),
                values_ref[i * C : (i + 1) * C, :],
                preferred_element_type=jnp.float32,
            )
        heads_ref[:, h * HD : (h + 1) * HD] = (mixed * share).astype(jnp.bfloat16)
    multiply_out(heads_ref, held_ref.at[0], sems.at[0], (), *outs[:parts])
    for i, out_ref in enumerate(outs[parts:], 1):
        multiply_out(heads_ref, held_ref.at[i], sems.at[i], (), out_ref)


def attend(r, column, plan, queries, old, new, o_weight, steps, parts):
    columns = HEADS * HD
    return pl.pallas_call(
        functools.partial(attend_kernel, r, steps, parts),
        out_shape=(rows_of(C, columns),)
        + (rows_of(C // parts, SHARD),) * parts
        + (rows_of(C, SHARD),) * (len(steps) - 1),
        in_specs=[SMEM] * 2 + [VMEM] * 5 + [HBM],
        out_specs=(VMEM,) * (parts + len(steps)),
        scratch_shapes=[
            pltpu.VMEM((len(steps), columns, SHARD), jnp.bfloat16),
            pltpu.VMEM((PRE + C, HD), jnp.bfloat16),
            pltpu.VMEM((PRE + C, HD), jnp.bfloat16),
            pltpu.SemaphoreType.DMA((len(steps), OUT_PARTS)),
        ],
        compiler_params=kernel_params(10 + 4 * len(steps)),
        cost_estimate=pl.CostEstimate(
            flops=4 * C * (PRE + C) * columns + 2 * len(steps) * C * columns * SHARD,
            bytes_accessed=(2 + 5 * len(steps)) * 2**20,
            transcendentals=C * (PRE + C) * HEADS,
        ),
        name=f"attend_{r}",
    )(column, plan, queries, *old, *new, o_weight)


def output_kernel(steps, column_ref, heads_ref, weight_ref, *refs):
    outs, (held_ref, sems) = refs[-2 - len(steps) : -2], refs[-2:]
    addends = refs[: -2 - len(steps)]
    for i, step in enumerate(steps):
        start_all(weight_copies(weight_ref, held_ref.at[i], column_ref[0] ^ step, sems.at[i]))
    for i, out_ref in enumerate(outs):
        multiply_out(heads_ref, held_ref.at[i], sems.at[i], addends, out_ref)


def output_blocks(column, heads, o_weight, steps, addends=(), dtype=jnp.bfloat16):
    return pl.pallas_call(
        functools.partial(output_kernel, steps),
        out_shape=(rows_of(C, SHARD, dtype=dtype),) * len(steps),
        in_specs=[SMEM, VMEM, HBM] + [VMEM] * len(addends),
        out_specs=(VMEM,) * len(steps),
        scratch_shapes=[
            pltpu.VMEM((len(steps), HEADS * HD, SHARD), jnp.bfloat16),
            pltpu.SemaphoreType.DMA((len(steps), OUT_PARTS)),
        ],
        compiler_params=kernel_params(8 + 4 * len(steps)),
        cost_estimate=QUICK,
        name="output_" + "".join(map(str, steps)),
    )(column, heads, o_weight, *addends)


def add_kernel(across_ref, *refs):
    parts, outs = refs[:ADD_PARTS], refs[ADD_PARTS:]
    height = C // ADD_PARTS
    for i, ref in enumerate(parts):
        rows = slice(i * height, (i + 1) * height)
        total = across_ref[rows, :].astype(jnp.float32) + ref[...].astype(jnp.float32)
        first = i * height % outs[0].shape[0]
        out_ref = outs[i * height // outs[0].shape[0]]
        out_ref[first : first + height, :] = total.astype(jnp.bfloat16)


def add_parts(across, parts, pieces):
    return pl.pallas_call(
        add_kernel,
        out_shape=(rows_of(C // pieces, SHARD),) * pieces,
        in_specs=[VMEM] * (1 + len(parts)),
        out_specs=(VMEM,) * pieces,
        compiler_params=kernel_params(8),
        cost_estimate=QUICK,
        name="add",
    )(across, *parts)


def finish_kernel(r, whole, split, plan_ref, *refs):
    held_ref, sems = refs[-2:]
    out_ref = refs[-3]
    slot = plan_ref[2 + r]
    copies = []
    for half in range(2):
        here = slice(half * HALF, (half + 1) * HALF)
        total = sum(ref[here, :].astype(jnp.float32) for ref in refs[:whole])
        for ref in refs[whole : whole + split * (half + 1)][split * half :]:
            total += ref[...].astype(jnp.float32)
        held_ref[here, :] = total.astype(jnp.bfloat16)
        copies += start_all(
            [
                pltpu.make_async_copy(
                    held_ref.at[pl.ds(half * HALF, HALF)],
                    out_ref.at[slot, pl.ds(half * HALF, HALF)],
                    sems.at[half],
                )
            ]
        )
    for copy in copies:
        copy.wait()


def finish(r, plan, addends, halves, hidden):
    earlier = [] if hidden is None else [hidden]
    operands = (plan, *addends, *halves, *earlier)
    return pl.pallas_call(
        functools.partial(finish_kernel, r, len(addends), len(halves) // 2),
        out_shape=rows_of(MAXW, C, SHARD),
        in_specs=[SMEM] + [VMEM] * (len(addends) + len(halves)) + [ANY] * len(earlier),
        out_specs=ANY,
        scratch_shapes=[pltpu.VMEM((C, SHARD), jnp.bfloat16), pltpu.SemaphoreType.DMA((2,))],
        input_output_aliases={len(operands) - 1: 0} if earlier else {},
        compiler_params=kernel_params(8),
        cost_estimate=QUICK,
        name=f"finish_{r}",
    )(*operands)


def pages_kernel(group_ref, counts_ref, destinations_ref, owner_ref, plan_ref, *refs):
    sources, (out_ref, held_ref, filled_ref, sems) = refs[:-4], refs[-4:]
    copies = start_all(
        [
            pltpu.make_async_copy(source, held_ref.at[i], sems.at[i])
            for i, source in enumerate(sources)
        ]
    )
    out_ref[...] = jnp.zeros(out_ref.shape, out_ref.dtype)
    filled_ref[0] = 0
    group = group_ref[0]
    for copy in copies:
        copy.wait()

    def span(s, carry):
        @pl.when(s % (2 * MAXW) < counts_ref[s // (2 * MAXW)])
        def _():
            target = destinations_ref[s]
            holder = target // MAXW
            place = jnp.where(plan_ref[8 + holder] == target % MAXW, 0, 1)
            away = jnp.where(group < holder, group - holder + GROUPS, group - holder)
            for i in range(C // PAGE):
                @pl.when(owner_ref[s * (C // PAGE) + i] == group)
                def _():
                    rank = filled_ref[0]
                    filled_ref[0] = rank + 1
                    out_ref[jnp.minimum(rank, OWNCAP - 1)] = held_ref[
                        away, place, i * PAGE : (i + 1) * PAGE, :
                    ]

        return carry

    lax.fori_loop(0, GROUPS * 2 * MAXW, span, 0)


def place_pages(group, counts, destinations, page_owner, plan, gathered):
    return pl.pallas_call(
        pages_kernel,
        out_shape=rows_of(OWNCAP, PAGE, SLICE),
        in_specs=[SMEM] * 5 + [ANY] * len(gathered),
        out_specs=VMEM,
        scratch_shapes=[
            pltpu.VMEM((GROUPS, 2, C, SLICE), jnp.bfloat16),
            pltpu.SMEM((1,), jnp.int32),
            pltpu.SemaphoreType.DMA((GROUPS,)),
        ],
        cost_estimate=QUICK,
        name="pages",
    )(group, counts, destinations, page_owner, plan, *gathered)


def stay(weight):
    return pltpu.with_memory_space_constraint(weight, pltpu.HBM)


def after(rows, other):
    return lax.optimization_barrier((rows, other))[0]


def routed_layer(
    tokens,
    prefix_kv,
    counts,
    destinations,
    page_owner,
    prefix_len,
    ln_gain,
    q_weight,
    q_bias,
    kv_weight,
    kv_bias,
    o_weight,
):
    group = lax.axis_index("pg").reshape(1)
    column = lax.axis_index("tp")
    columns = column.reshape(1)
    plan, *choices, leave_first, leave_second = route(
        group, counts, destinations, prefix_len, tokens, prefix_kv
    )
    gain = ln_gain.astype(jnp.float32).reshape(KVH, 1, SHARD)
    q_blocks = stay(q_weight.reshape(KVH, SHARD, HEADS * HD))
    kv_blocks = stay(kv_weight.reshape(KVH, SHARD, SLICE))
    o_weight = stay(o_weight)
    q_row, kv_row = q_bias.reshape(1, -1), kv_bias.reshape(1, -1)
    tables = [stay(table) for table in rope_tables()]
    keeps_own = (column == 0) | (column == KVH - 1)

    def swap(rows, step):
        return lax.ppermute(rows, "tp", [(i, i ^ step) for i in range(KVH)])

    def share_head(mine, other):
        passed = swap(other, 1)
        return jnp.where(keeps_own, mine, passed), jnp.where(keeps_own, passed, mine)

    def rotate_groups(rows):
        return [
            lax.ppermute(rows, "pg", [(i, (i + step) % GROUPS) for i in range(GROUPS)])
            for step in range(1, GROUPS)
        ]

    def add_pair(a, b):
        return (a.astype(jnp.float32) + b.astype(jnp.float32)).astype(jnp.bfloat16)

    def first_round(pairs, leaving):
        return lax.ppermute(leaving, "pg", pairs)

    def second_round(pairs, leaving, rows):
        across = swap(rows, 2)
        return lax.ppermute(leaving, "pg", pairs), swap(rows, 1), across, swap(across, 1)

    patterns = round_patterns()
    arrived = lax.switch(
        choices[0][0], [functools.partial(first_round, pairs) for pairs in patterns], leave_first
    )
    rows_0, *old_0 = settle(0, columns, plan, tokens, prefix_kv, arrived)
    leave_second, rows_0 = lax.optimization_barrier((leave_second, rows_0))
    arrived, *others_0 = lax.switch(
        choices[1][0],
        [functools.partial(second_round, pairs) for pairs in patterns],
        leave_second,
        rows_0,
    )
    rows_1, *old_1, top_rows_1, bottom_rows_1 = settle(
        1, columns, plan, tokens, prefix_kv, arrived
    )
    others_0, old_0, rows_1 = lax.optimization_barrier((others_0, old_0, rows_1))

    beside_1 = swap(rows_1, 1)
    top_1 = swap(top_rows_1, 2)
    old_kept_0, old_crossing_0 = share_head(*old_0)
    pieces = [[rows_0]] + [[rows] for rows in others_0]
    normed, fresh_0, *new_0 = fresh_rows(
        0, columns, plan, pieces, gain, kv_blocks, kv_row, tables
    )
    new_kept_0, new_crossing_0 = share_head(*new_0)
    old_crossed_0 = swap(after(old_crossing_0, fresh_0), 2)
    new_crossed_0 = swap(new_crossing_0, 2)
    queries = query_rows(0, plan, after(normed, beside_1), q_blocks, q_row, tables)
    bottom_1 = swap(after(bottom_rows_1, queries), 2)
    old_kept_1, old_crossing_1 = share_head(*old_1)
    old_crossed_1 = swap(after(old_crossing_1, fresh_0), 2)
    _, *corner, beside_0, across, kept_0 = attend(
        0, columns, plan, after(queries, (top_1, old_crossed_1)), (old_kept_0, old_crossed_0),
        (new_kept_0, new_crossed_0), o_weight, (3, 1, 2, 0), ADD_PARTS,
    )
    corner = [swap(rows, 1) for rows in after(corner, bottom_1)]
    sum_top, sum_bottom = add_parts(across, corner, 2)
    total_top = swap(sum_top, 2)
    passed_0 = swap(beside_0, 1)

    pieces = [[after(rows_1, sum_top)], [beside_1], [top_1, bottom_1]]
    pieces.append([swap(rows, 1) for rows in pieces[2]])
    normed, fresh_1, *new_1 = fresh_rows(
        1, columns, plan, pieces, gain, kv_blocks, kv_row, tables
    )
    new_kept_1, new_crossing_1 = share_head(*new_1)
    new_crossed_1 = swap(new_crossing_1, 2)
    queries = query_rows(1, plan, after(normed, passed_0), q_blocks, q_row, tables)
    heads, *corner = attend(
        1, columns, plan, after(queries, total_top), (old_kept_1, old_crossed_1),
        (new_kept_1, new_crossed_1), o_weight, (3,), ADD_PARTS,
    )
    total_bottom = swap(after(sum_bottom, heads), 2)
    corner = [swap(rows, 1) for rows in corner]
    across, beside_1 = output_blocks(columns, heads, o_weight, (2, 1))
    (sum_all,) = add_parts(across, corner, 1)
    sum_all = after(sum_all, total_bottom)
    total_1 = swap(sum_all, 2)

    fresh = jnp.stack([fresh_0, after(fresh_1, sum_all)])
    gathered = [fresh] + rotate_groups(fresh)
    passed_1 = swap(after(beside_1, sum_all), 1)
    (base_1,) = output_blocks(
        columns, after(heads, sum_all), o_weight, (0,), (rows_1, passed_1), jnp.float32
    )
    hidden = finish(
        0, plan, (rows_0, kept_0, after(passed_0, sum_all)), (total_top, total_bottom), None
    )
    hidden = finish(1, plan, (base_1, total_1), (), hidden)
    kv_pages = place_pages(
        group, counts, destinations, page_owner, plan, after(gathered, hidden)
    )
    return (hidden, kv_pages)


def gathered_layer(
    tokens,
    prefix_kv,
    counts,
    destinations,
    page_owner,
    prefix_len,
    ln_gain,
    q_weight,
    q_bias,
    kv_weight,
    kv_bias,
    o_weight,
):
    groups = lax.axis_size("pg")
    group_index = lax.axis_index("pg")
    column = lax.axis_index("tp")
    source_count = tokens.shape[0]
    heads_here = q_weight.shape[1] // HD
    group_size = HQ // KVH
    local_kv_heads = max(1, heads_here // group_size)
    first_kv_head = column * heads_here // group_size
    slice_width = prefix_kv.shape[2]
    extra_slots = source_count - MAXW
    source, filled, is_valid = work_sources(counts, destinations, groups)
    rank_table = page_ranks(is_valid, page_owner, groups)
    own_sources = lax.dynamic_slice_in_dim(source, group_index * MAXW, MAXW)
    stays_home = jnp.arange(MAXW, dtype=jnp.int32) < counts[group_index]
    spare_index = jnp.arange(groups * extra_slots, dtype=jnp.int32)
    spare_slot = spare_index // extra_slots * source_count + MAXW + spare_index % extra_slots
    spare_valid = MAXW + spare_index % extra_slots < counts[spare_index // extra_slots]
    wanted = group_index * MAXW + jnp.arange(MAXW, dtype=jnp.int32)
    matches = spare_valid[None, :] & (destinations[spare_slot][None, :] == wanted[:, None])
    chosen = jnp.sum(jnp.where(matches, spare_index[None, :], 0), axis=1)

    def settle(own_rows, moved_rows):
        return jnp.where(stays_home[:, None, None], own_rows, moved_rows[chosen])

    gathered = lax.all_gather(prefix_kv, "tp", axis=2, tiled=True)
    head_columns = head_block(gathered, first_kv_head, local_kv_heads)
    moved_tokens, moved_heads = (
        lax.all_gather(tokens[MAXW:], "pg", axis=0, tiled=True),
        lax.all_gather(head_columns[MAXW:], "pg", axis=0, tiled=True),
    )
    work_tokens = settle(tokens[:MAXW], moved_tokens)
    work_prefix = settle(head_columns[:MAXW], moved_heads)
    features = lax.all_gather(work_tokens, "tp", axis=2, tiled=True)
    feature_rows = features.astype(jnp.float32)
    inv_rms = lax.rsqrt(jnp.mean(feature_rows * feature_rows, axis=-1, keepdims=True) + norm_eps)
    normed = (feature_rows * inv_rms * ln_gain.astype(jnp.float32)).astype(jnp.bfloat16)
    flat_normed = normed.reshape(MAXW * C, D)
    queries = jnp.dot(flat_normed, q_weight, preferred_element_type=jnp.float32) + q_bias.astype(
        jnp.float32
    )
    fresh_columns = (
        jnp.dot(flat_normed, kv_weight, preferred_element_type=jnp.float32)
        + kv_bias.astype(jnp.float32)
    ).astype(jnp.bfloat16)
    fresh_all = lax.all_gather(
        fresh_columns.reshape(MAXW, C, slice_width), "tp", axis=2, tiled=True
    )
    prefix_start = prefix_len[own_sources]
    positions = prefix_start[:, None] + jnp.arange(C, dtype=jnp.int32)[None, :]
    cosine, sine_table = rope_angles(positions)
    cosine = cosine[:, :, None, :]
    sine_table = sine_table[:, :, None, :]
    queries = (
        rotate(queries.reshape(MAXW, C, heads_here, HD), cosine, sine_table) * HD ** (-0.5)
    ).astype(jnp.bfloat16)
    fresh_all = fresh_all.reshape(MAXW, C, 2, KVH, HD)
    new_keys = rotate(fresh_all[:, :, 0].astype(jnp.float32), cosine, sine_table).astype(
        jnp.bfloat16
    )
    new_kv = jnp.concatenate(
        [new_keys.reshape(MAXW, C, KVH * HD), fresh_all[:, :, 1].reshape(MAXW, C, KVH * HD)], axis=2
    )
    new_heads = head_block(new_kv, first_kv_head, local_kv_heads)
    all_rows = jnp.concatenate([work_prefix, new_heads], axis=1).reshape(
        MAXW, PRE + C, 2, local_kv_heads, HD
    )
    key_rows = all_rows[:, :, 0]
    value_rows = all_rows[:, :, 1]
    grouped = queries.reshape(MAXW, C, local_kv_heads, heads_here // local_kv_heads, HD)
    scores = jnp.einsum("wcngd,wlnd->wngcl", grouped, key_rows, preferred_element_type=jnp.float32)
    key_index = jnp.arange(PRE + C, dtype=jnp.int32)
    query_row = jnp.arange(C, dtype=jnp.int32)
    allowed = jnp.where(
        key_index[None, None, :] < PRE,
        key_index[None, None, :] < prefix_start[:, None, None],
        (key_index - PRE)[None, None, :] <= query_row[None, :, None],
    )
    scores = jnp.where(allowed[:, None, None], scores, -jnp.inf)
    row_max = jnp.max(scores, axis=-1, keepdims=True)
    weights = jnp.exp(scores - row_max)
    probabilities = (weights / jnp.sum(weights, axis=-1, keepdims=True)).astype(jnp.bfloat16)
    mixed_heads = jnp.einsum(
        "wngcl,wlnd->wcngd", probabilities, value_rows, preferred_element_type=jnp.float32
    ).astype(jnp.bfloat16)
    head_partial = jnp.dot(
        mixed_heads.reshape(MAXW * C, heads_here * HD), o_weight, preferred_element_type=jnp.float32
    ).reshape(MAXW, C, D)
    attended = lax.psum_scatter(
        head_partial.astype(jnp.bfloat16), "tp", scatter_dimension=2, tiled=True
    ).astype(jnp.float32)
    hidden = (work_tokens.astype(jnp.float32) + attended).astype(jnp.bfloat16)
    pages_per = C // PAGE
    own_columns = lax.dynamic_slice_in_dim(new_kv, column * slice_width, slice_width, 2)
    page_rows = own_columns.reshape(MAXW * pages_per, PAGE, slice_width)
    work_page = jnp.arange(groups * MAXW * pages_per, dtype=jnp.int32)
    source_page = source[work_page // pages_per] * pages_per + work_page % pages_per
    owner_of_page = page_owner[source_page]
    local_owner = lax.dynamic_slice_in_dim(
        owner_of_page, group_index * MAXW * pages_per, MAXW * pages_per
    )
    addressed = local_owner[None, :] == jnp.arange(groups, dtype=jnp.int32)[:, None]
    outbox = jnp.where(addressed[:, :, None, None], page_rows[None], jnp.zeros((), jnp.bfloat16))
    arrived = lax.all_to_all(outbox, "pg", split_axis=0, concat_axis=0, tiled=True).reshape(
        groups * MAXW * pages_per, PAGE, slice_width
    )
    retained = filled[work_page // pages_per] & (owner_of_page == group_index)
    slot_matches = retained[None, :] & (
        rank_table[source_page][None, :] == jnp.arange(OWNCAP, dtype=jnp.int32)[:, None]
    )
    slot_pick = jnp.sum(jnp.where(slot_matches, work_page[None, :], 0), axis=1)
    kv_pages = jnp.where(
        jnp.any(slot_matches, axis=1)[:, None, None],
        arrived[slot_pick],
        jnp.zeros((), jnp.bfloat16),
    )
    return (hidden, kv_pages)


def solution(mesh):
    in_specs = (
        P(("parts", "pg"), None, "tp"),
        P(("parts", "pg"), None, "tp"),
        P("parts"),
        P("parts"),
        P("parts"),
        P("parts"),
        P(),
        P(None, "tp"),
        P("tp"),
        P(None, "tp"),
        P("tp"),
        P("tp", None),
    )
    out_specs = (P(("parts", "pg"), None, "tp"), P(("parts", "pg"), None, "tp"))
    if mesh.shape["pg"] == 4 and mesh.shape["tp"] == KVH:
        layer = routed_layer
    else:
        layer = gathered_layer
    return jax.shard_map(layer, mesh=mesh, in_specs=in_specs, out_specs=out_specs, check_vma=False)
```

```python
import functools
import itertools

import jax
import jax.numpy as jnp
import numpy as np
from jax import lax
from jax.experimental import pallas as pl
from jax.experimental.pallas import tpu as pltpu
from jax.sharding import PartitionSpec as P

D = 8192
HQ = 32
KVH = 4
HD = 128
C = 256
PRE = 512
MAXW = 2
PAGE = 64
OWNCAP = 16


rope_base = 1000000.0
norm_eps = 1e-06


def work_sources(counts, destinations, groups):
    source_count = 2 * MAXW
    source_slot = jnp.arange(groups * source_count, dtype=jnp.int32)
    is_valid = source_slot % source_count < counts[source_slot // source_count]
    work_slot = jnp.arange(groups * MAXW, dtype=jnp.int32)
    matches = is_valid[None, :] & (destinations[None, :] == work_slot[:, None])
    source = jnp.sum(jnp.where(matches, source_slot[None, :], 0), axis=1)
    filled = jnp.any(matches, axis=1)
    return (source, filled, is_valid)


def page_ranks(is_valid, page_owner, groups):
    pages_per = C // PAGE
    page_valid = jnp.repeat(is_valid, pages_per)
    membership = (
        page_valid[:, None] & (page_owner[:, None] == jnp.arange(groups, dtype=jnp.int32)[None, :])
    ).astype(jnp.int32)
    earlier_count = jnp.cumsum(membership, axis=0) - membership
    return jnp.sum(earlier_count * membership, axis=1)


def rope_angles(positions):
    half_dim = HD // 2
    frequency = rope_base ** (-(jnp.arange(half_dim, dtype=jnp.float32) * (2.0 / HD)))
    angles = positions.astype(jnp.float32)[..., None] * frequency
    return (jnp.cos(angles), jnp.sin(angles))


def rotate(vectors, cosine, sine_table):
    half_dim = HD // 2
    first_half = vectors[..., :half_dim]
    second_half = vectors[..., half_dim:]
    return jnp.concatenate(
        [
            first_half * cosine - second_half * sine_table,
            second_half * cosine + first_half * sine_table,
        ],
        axis=-1,
    )


def head_block(rows, first_head, head_count):
    key_part = lax.dynamic_slice_in_dim(rows, first_head * HD, head_count * HD, 2)
    value_part = lax.dynamic_slice_in_dim(rows, KVH * HD + first_head * HD, head_count * HD, 2)
    return jnp.concatenate([key_part, value_part], axis=2)


GROUPS = 4
SHARD = D // KVH
HEADS = HQ // KVH
SLICE = 2 * HD
HALF = C // 2
NORM_ROWS = 16
OUT_PARTS = 2
ADD_PARTS = 4
SMEM = pl.BlockSpec(memory_space=pltpu.SMEM)
VMEM = pl.BlockSpec(memory_space=pltpu.VMEM)
HBM = pl.BlockSpec(memory_space=pltpu.HBM)
ANY = pl.BlockSpec(memory_space=pl.ANY)
QUICK = pl.CostEstimate(flops=1, bytes_accessed=1, transcendentals=0)


def kernel_params(mib):
    return pltpu.CompilerParams(vmem_limit_bytes=mib * 2**20)


def rows_of(*shape, dtype=jnp.bfloat16):
    return jax.ShapeDtypeStruct(shape, dtype)


def start_all(copies):
    for copy in copies:
        copy.start()
    return copies


def rope_tables():
    frequency = rope_base ** (-(np.arange(HD // 2, dtype=np.float32) * np.float32(2.0 / HD)))
    positions = np.arange(PRE + C, dtype=np.float32)
    angles = positions[:, None] * frequency.astype(np.float32)
    cosine, sine = np.cos(angles), np.sin(angles)
    tables = (np.concatenate([cosine, cosine], 1), np.concatenate([-sine, sine], 1))
    return [jnp.asarray(t.astype(np.float32).reshape(-1, C, HD)) for t in tables]


def round_patterns():
    patterns = []
    for senders in itertools.combinations(range(GROUPS), 2):
        low, high = [g for g in range(GROUPS) if g not in senders]
        patterns.append([(senders[0], low), (senders[1], high)])
        patterns.append([(senders[0], high), (senders[1], low)])
    return patterns


def leave_copies(slot, tokens_ref, prefix_ref, leave_ref, sems):
    return [
        pltpu.make_async_copy(tokens_ref.at[slot], leave_ref.at[:, pl.ds(0, SHARD)], sems.at[0])
    ] + [
        pltpu.make_async_copy(
            prefix_ref.at[slot, pl.ds(half * C, C)],
            leave_ref.at[:, pl.ds(SHARD + half * SLICE, SLICE)],
            sems.at[1 + half],
        )
        for half in range(2)
    ]


def route_kernel(
    group_ref, counts_ref, destinations_ref, prefix_len_ref, tokens_ref, prefix_ref,
    plan_ref, first_ref, second_ref, leave_first, leave_second, table_ref, sems,
):
    group = group_ref[0]
    counts = [counts_ref[g] for g in range(GROUPS)]

    def pick(flags, default):
        found = jnp.int32(default)
        for g in reversed(range(GROUPS)):
            found = jnp.where(flags[g], g, found)
        return found

    full = pick([count == 2 * MAXW for count in counts], 0)
    other = pick([(counts[g] > MAXW) & (full != g) for g in range(GROUPS)], -1)
    other_group = jnp.maximum(other, 0)
    other_spare = jnp.where(other >= 0, counts_ref[other_group] - MAXW, 0)
    full_to = [destinations_ref[full * 4 + 2 + i] for i in range(2)]
    other_to = [destinations_ref[other_group * 4 + 2 + i] for i in range(2)]
    clash_first = (other_spare > 0) & (full_to[0] // MAXW == other_to[0] // MAXW)
    clash_second = (other_spare > 1) & (full_to[1] // MAXW == other_to[1] // MAXW)
    swapped = clash_first | clash_second
    moves, copies = [], []
    for r in range(2):
        a, b = full, full_to[r] // MAXW
        take = jnp.where(swapped, 1 - r, r)
        second = other_spare > take
        to = jnp.where(swapped, other_to[1 - r], other_to[r])
        c, d = other_group, to // MAXW
        free = jnp.where((a != 0) & (b != 0), 0, jnp.where((a != 1) & (b != 1), 1, 2))
        free_to = jnp.where(b > a, free, 6 - a - b - free)
        with_a = jnp.where(second, c, 6 - a - b - free_to)
        with_b = jnp.where(second, d, free_to)
        low, high = jnp.minimum(a, with_a), jnp.maximum(a, with_a)
        low_to = jnp.where(a < with_a, b, with_b)
        high_to = jnp.where(a < with_a, with_b, b)
        pair = jnp.where(low == 0, 0, jnp.where(low == 1, 3, 5)) + high - low - 1
        pattern = 2 * pair + (low_to > high_to).astype(jnp.int32)
        (first_ref, second_ref)[r][0] = pattern
        leaving = jnp.where((group == c) & second, 2 + take, 2 + r)
        leave_ref = (leave_first, leave_second)[r]
        copies += start_all(leave_copies(leaving, tokens_ref, prefix_ref, leave_ref, sems.at[r]))
        moves.append((a, b, full_to[r], 2 + r, second, c, d, to, 2 + take))
    for g in range(GROUPS):
        got, slots, origins = [], [], []
        for a, b, a_to, a_slot, second, c, d, c_to, c_slot in moves:
            from_full = b == g
            got.append(from_full | (second & (d == g)))
            slots.append(jnp.where(from_full, a_to, c_to) % MAXW)
            origins.append(jnp.where(from_full, a * 4 + a_slot, c * 4 + c_slot))
        for r in range(2):
            home_slot = jnp.where(got[1 - r], 1 - slots[1 - r], r)
            slot = jnp.where(got[r], slots[r], home_slot)
            table_ref[g * 8 + r] = jnp.where(got[r], 0, 1)
            table_ref[g * 8 + 2 + r] = slot
            table_ref[g * 8 + 4 + r] = prefix_len_ref[jnp.where(got[r], origins[r], g * 4 + slot)]
            if r == 0:
                plan_ref[8 + g] = slot
    for i in range(6):
        plan_ref[i] = table_ref[group * 8 + i]
    for copy in copies:
        copy.wait()


def route(group, counts, destinations, prefix_len, tokens, prefix_kv):
    leaving = rows_of(C, SHARD + 2 * SLICE)
    one = rows_of(1, dtype=jnp.int32)
    return pl.pallas_call(
        route_kernel,
        out_shape=(rows_of(16, dtype=jnp.int32), one, one, leaving, leaving),
        in_specs=[SMEM] * 4 + [ANY] * 2,
        out_specs=(SMEM, SMEM, SMEM, VMEM, VMEM),
        scratch_shapes=[
            pltpu.SMEM((GROUPS * 8,), jnp.int32),
            pltpu.SemaphoreType.DMA((2, 3)),
        ],
        cost_estimate=QUICK,
        name="route",
    )(group, counts, destinations, prefix_len, tokens, prefix_kv)


def settle_kernel(
    r, column_ref, plan_ref, tokens_ref, prefix_ref, arrived_ref, rows_ref, mine_ref, other_ref, *refs
):
    halves_of_rows, sems = refs[:-1], refs[-1]
    at_home = plan_ref[r] == 1
    slot = plan_ref[2 + r]
    odd = column_ref[0] % 2
    halves = [(half, part) for half in range(PRE // C) for part in range(2)]

    def token_copies(source):
        whole = [pltpu.make_async_copy(source, rows_ref, sems.at[0])]
        return whole + [
            pltpu.make_async_copy(source.at[pl.ds(half * HALF, HALF)], ref, sems.at[5 + half])
            for half, ref in enumerate(halves_of_rows)
        ]

    def head(half, part):
        target = (mine_ref, other_ref)[part].at[pl.ds(half * C, C)]
        side = pl.multiple_of(jnp.where(odd == part, 0, HD), HD)
        return target, side

    @pl.when(at_home)
    def _():
        start_all(token_copies(tokens_ref.at[slot]))
        for i, (half, part) in enumerate(halves):
            target, side = head(half, part)
            source = prefix_ref.at[slot, pl.ds(half * C, C), pl.ds(side, HD)]
            pltpu.make_async_copy(source, target, sems.at[1 + i]).start()

    moved = token_copies(arrived_ref.at[:, pl.ds(0, SHARD)])
    for i, (half, part) in enumerate(halves):
        target, side = head(half, part)
        place = pl.multiple_of(SHARD + half * SLICE + side, HD)
        source = arrived_ref.at[:, pl.ds(place, HD)]
        moved.append(pltpu.make_async_copy(source, target, sems.at[1 + i]))

    @pl.when(jnp.logical_not(at_home))
    def _():
        start_all(moved)

    for copy in moved:
        copy.wait()


def settle(r, column, plan, tokens, prefix_kv, arrived):
    return pl.pallas_call(
        functools.partial(settle_kernel, r),
        out_shape=(rows_of(C, SHARD), rows_of(PRE, HD), rows_of(PRE, HD))
        + (rows_of(HALF, SHARD),) * (2 * r),
        in_specs=[SMEM] * 2 + [ANY] * 3,
        out_specs=(VMEM,) * (3 + 2 * r),
        scratch_shapes=[pltpu.SemaphoreType.DMA((3 + 2 * (PRE // C),))],
        cost_estimate=QUICK,
        name=f"settle_{r}",
    )(column, plan, tokens, prefix_kv, arrived)


def turn(block, cosine, sine):
    return block * cosine + pltpu.roll(block, HD // 2, 1) * sine


def table_copies(r, plan_ref, tables, held_ref, sems):
    block = plan_ref[4 + r] // C
    return [
        pltpu.make_async_copy(table.at[block], held_ref.at[i], sems.at[i])
        for i, table in enumerate(tables)
    ]


def fresh_kernel(r, split, column_ref, plan_ref, gain_ref, bias_ref, *refs):
    pieces, refs = refs[: sum(split)], refs[sum(split) :]
    cos_ref, sin_ref, weight_ref, normed_ref, fresh_ref, mine_ref, other_ref = refs[:7]
    held_ref, turn_ref, sems, turn_sems = refs[7:]
    column = column_ref[0]
    copies = start_all(
        [pltpu.make_async_copy(weight_ref.at[k], held_ref.at[k], sems.at[k]) for k in range(KVH)]
    )
    turns = start_all(table_copies(r, plan_ref, (cos_ref, sin_ref), turn_ref, turn_sems))

    for half in range(2):
        sources, at = [], 0
        for parts in split:
            sources.append((pieces[at + half], 0) if parts == 2 else (pieces[at], half * HALF))
            at += parts

        def rows(i, carry):
            start = i * NORM_ROWS
            blocks = [
                (ref, pl.ds(pl.multiple_of(first + start, NORM_ROWS), NORM_ROWS))
                for ref, first in sources
            ]
            total = jnp.zeros((NORM_ROWS, HD), jnp.float32)
            for ref, here in blocks:
                for j in range(SHARD // HD):
                    x = ref[here, j * HD : (j + 1) * HD].astype(jnp.float32)
                    total += x * x
            inv_rms = lax.rsqrt(jnp.sum(total, axis=1, keepdims=True) * (1.0 / D) + norm_eps)
            there = pl.ds(pl.multiple_of(half * HALF + start, NORM_ROWS), NORM_ROWS)
            for k, (ref, here) in enumerate(blocks):
                owner = column ^ k
                x = ref[here, :].astype(jnp.float32)
                normed_ref[owner, there, :] = (x * inv_rms * gain_ref[owner]).astype(jnp.bfloat16)
            return carry

        lax.fori_loop(0, HALF // NORM_ROWS, rows, 0, unroll=4)
    terms = []
    for k in range(KVH):
        copies[k].wait()
        terms.append(jnp.dot(normed_ref[k], held_ref[k], preferred_element_type=jnp.float32))
    total = (terms[0] + terms[1]) + (terms[2] + terms[3])
    fresh = (total + bias_ref[...].astype(jnp.float32)).astype(jnp.bfloat16)
    for copy in turns:
        copy.wait()
    is_key = column < KVH // 2
    blocks = []
    for h in range(2):
        block = fresh[:, h * HD : (h + 1) * HD]
        turned = turn(block.astype(jnp.float32), turn_ref[0], turn_ref[1]).astype(jnp.bfloat16)
        blocks.append(jnp.where(is_key, turned, block))
        fresh_ref[:, h * HD : (h + 1) * HD] = blocks[h]
    odd = column % 2 == 1
    mine_ref[...] = jnp.where(odd, blocks[1], blocks[0])
    other_ref[...] = jnp.where(odd, blocks[0], blocks[1])


def fresh_rows(r, column, plan, pieces, gain, kv_weight, kv_bias, tables):
    flat = [part for piece in pieces for part in piece]
    head = rows_of(C, HD)
    return pl.pallas_call(
        functools.partial(fresh_kernel, r, [len(piece) for piece in pieces]),
        out_shape=(rows_of(KVH, C, SHARD), rows_of(C, SLICE), head, head),
        in_specs=[SMEM] * 2 + [VMEM] * (2 + len(flat)) + [HBM] * 3,
        out_specs=(VMEM,) * 4,
        scratch_shapes=[
            pltpu.VMEM((KVH, SHARD, SLICE), jnp.bfloat16),
            pltpu.VMEM((2, C, HD), jnp.float32),
            pltpu.SemaphoreType.DMA((KVH,)),
            pltpu.SemaphoreType.DMA((2,)),
        ],
        compiler_params=kernel_params(16),
        cost_estimate=QUICK,
        name=f"fresh_{r}",
    )(column, plan, gain, kv_bias, *flat, *tables, kv_weight)


def query_kernel(
    r, plan_ref, normed_ref, bias_ref, cos_ref, sin_ref, weight_ref,
    out_ref, held_ref, total_ref, turn_ref, sems, turn_sems,
):
    depth = SHARD // 2
    start_all(
        [
            pltpu.make_async_copy(
                weight_ref.at[i // 2, pl.ds(i % 2 * depth, depth)], held_ref.at[i], sems.at[i]
            )
            for i in range(2 * KVH)
        ]
    )
    turns = start_all(table_copies(r, plan_ref, (cos_ref, sin_ref), turn_ref, turn_sems))
    total_ref[...] = jnp.broadcast_to(bias_ref[...].astype(jnp.float32), total_ref.shape)

    def add_term(i, carry):
        pltpu.make_async_copy(held_ref.at[i], held_ref.at[i], sems.at[i]).wait()
        here = pl.ds(pl.multiple_of(i % 2 * depth, depth), depth)
        total_ref[...] += jnp.dot(
            normed_ref[i // 2, :, here], held_ref[i], preferred_element_type=jnp.float32
        )
        return carry

    lax.fori_loop(0, 2 * KVH, add_term, 0)
    for copy in turns:
        copy.wait()
    for h in range(HEADS):
        here = slice(h * HD, (h + 1) * HD)
        block = turn(total_ref[:, here], turn_ref[0], turn_ref[1])
        out_ref[:, here] = (block * HD ** (-0.5)).astype(jnp.bfloat16)


def query_rows(r, plan, normed, q_weight, q_bias, tables):
    columns = HEADS * HD
    return pl.pallas_call(
        functools.partial(query_kernel, r),
        out_shape=rows_of(C, columns),
        in_specs=[SMEM] + [VMEM] * 2 + [HBM] * 3,
        out_specs=VMEM,
        scratch_shapes=[
            pltpu.VMEM((2 * KVH, SHARD // 2, columns), jnp.bfloat16),
            pltpu.VMEM((C, columns), jnp.float32),
            pltpu.VMEM((2, C, HD), jnp.float32),
            pltpu.SemaphoreType.DMA((2 * KVH,)),
            pltpu.SemaphoreType.DMA((2,)),
        ],
        compiler_params=kernel_params(24),
        cost_estimate=QUICK,
        name=f"queries_{r}",
    )(plan, normed, q_bias, *tables, q_weight)


def weight_copies(weight_ref, held_ref, block, sems):
    width = SHARD // OUT_PARTS
    return [
        pltpu.make_async_copy(
            weight_ref.at[:, pl.ds(pl.multiple_of(block * SHARD + i * width, width), width)],
            held_ref.at[:, pl.ds(i * width, width)],
            sems.at[i],
        )
        for i in range(OUT_PARTS)
    ]


def multiply_out(rows_ref, held_ref, sems, addends, *outs):
    width = SHARD // OUT_PARTS

    def part(i, carry):
        here = pl.ds(pl.multiple_of(i * width, width), width)
        pltpu.make_async_copy(held_ref.at[:, here], held_ref.at[:, here], sems.at[i]).wait()
        total = jnp.dot(rows_ref[...], held_ref[:, here], preferred_element_type=jnp.float32)
        for ref in addends:
            total += ref[:, here].astype(jnp.float32)
        for k, ref in enumerate(outs):
            height = ref.shape[0]
            ref[:, here] = total[k * height : (k + 1) * height].astype(ref.dtype)
        return carry

    lax.fori_loop(0, OUT_PARTS, part, 0)


def attend_kernel(r, steps, parts, column_ref, plan_ref, query_ref, *refs):
    old_kept, old_crossed, new_kept, new_crossed, weight_ref, heads_ref = refs[:6]
    outs, (held_ref, keys_ref, values_ref, sems) = refs[6:-4], refs[-4:]
    column = column_ref[0]
    for i, step in enumerate(steps):
        start_all(weight_copies(weight_ref, held_ref.at[i], column ^ step, sems.at[i]))
    upper = column >= KVH // 2
    for rows, kept, crossed in ((pl.ds(0, PRE), old_kept, old_crossed), (pl.ds(PRE, C), new_kept, new_crossed)):
        keys_ref[rows, :] = jnp.where(upper, crossed[...], kept[...])
        values_ref[rows, :] = jnp.where(upper, kept[...], crossed[...])
    seen = [
        jnp.where(plan_ref[4 + r] > i * C, 0.0, -jnp.inf).astype(jnp.float32)
        for i in range(PRE // C)
    ]
    causal = lax.broadcasted_iota(jnp.int32, (C, C), 1) <= lax.broadcasted_iota(
        jnp.int32, (C, C), 0
    )
    key_blocks = range(PRE // C + 1)

    def score(h):
        query = query_ref[:, h * HD : (h + 1) * HD]
        scores = lax.dot_general(
            query, keys_ref[...], (((1,), (1,)), ((), ())), preferred_element_type=jnp.float32
        )
        return [scores[:, i * C : (i + 1) * C] for i in key_blocks]

    upcoming = score(0)
    for h in range(HEADS):
        blocks = upcoming
        if h + 1 < HEADS:
            upcoming = score(h + 1)
        blocks = [block + bias for block, bias in zip(blocks, seen)] + [
            jnp.where(causal, blocks[-1], -jnp.inf)
        ]
        top = jnp.max(functools.reduce(jnp.maximum, blocks), axis=1, keepdims=True)
        blocks = [jnp.exp(block - top) for block in blocks]
        share = 1.0 / jnp.sum(functools.reduce(jnp.add, blocks), axis=1, keepdims=True)
        mixed = jnp.zeros((C, HD), jnp.float32)
        for i in key_blocks:
            mixed += jnp.dot(
                blocks[i].astype(jnp.bfloat16),
                values_ref[i * C : (i + 1) * C, :],
                preferred_element_type=jnp.float32,
            )
        heads_ref[:, h * HD : (h + 1) * HD] = (mixed * share).astype(jnp.bfloat16)
    multiply_out(heads_ref, held_ref.at[0], sems.at[0], (), *outs[:parts])
    for i, out_ref in enumerate(outs[parts:], 1):
        multiply_out(heads_ref, held_ref.at[i], sems.at[i], (), out_ref)


def attend(r, column, plan, queries, old, new, o_weight, steps, parts):
    columns = HEADS * HD
    return pl.pallas_call(
        functools.partial(attend_kernel, r, steps, parts),
        out_shape=(rows_of(C, columns),)
        + (rows_of(C // parts, SHARD),) * parts
        + (rows_of(C, SHARD),) * (len(steps) - 1),
        in_specs=[SMEM] * 2 + [VMEM] * 5 + [HBM],
        out_specs=(VMEM,) * (parts + len(steps)),
        scratch_shapes=[
            pltpu.VMEM((len(steps), columns, SHARD), jnp.bfloat16),
            pltpu.VMEM((PRE + C, HD), jnp.bfloat16),
            pltpu.VMEM((PRE + C, HD), jnp.bfloat16),
            pltpu.SemaphoreType.DMA((len(steps), OUT_PARTS)),
        ],
        compiler_params=kernel_params(10 + 4 * len(steps)),
        cost_estimate=pl.CostEstimate(
            flops=4 * C * (PRE + C) * columns + 2 * len(steps) * C * columns * SHARD,
            bytes_accessed=(2 + 5 * len(steps)) * 2**20,
            transcendentals=C * (PRE + C) * HEADS,
        ),
        name=f"attend_{r}",
    )(column, plan, queries, *old, *new, o_weight)


def output_kernel(steps, column_ref, heads_ref, weight_ref, *refs):
    outs, (held_ref, sems) = refs[-2 - len(steps) : -2], refs[-2:]
    addends = refs[: -2 - len(steps)]
    for i, step in enumerate(steps):
        start_all(weight_copies(weight_ref, held_ref.at[i], column_ref[0] ^ step, sems.at[i]))
    for i, out_ref in enumerate(outs):
        multiply_out(heads_ref, held_ref.at[i], sems.at[i], addends, out_ref)


def output_blocks(column, heads, o_weight, steps, addends=(), dtype=jnp.bfloat16):
    return pl.pallas_call(
        functools.partial(output_kernel, steps),
        out_shape=(rows_of(C, SHARD, dtype=dtype),) * len(steps),
        in_specs=[SMEM, VMEM, HBM] + [VMEM] * len(addends),
        out_specs=(VMEM,) * len(steps),
        scratch_shapes=[
            pltpu.VMEM((len(steps), HEADS * HD, SHARD), jnp.bfloat16),
            pltpu.SemaphoreType.DMA((len(steps), OUT_PARTS)),
        ],
        compiler_params=kernel_params(8 + 4 * len(steps)),
        cost_estimate=QUICK,
        name="output_" + "".join(map(str, steps)),
    )(column, heads, o_weight, *addends)


def add_kernel(across_ref, *refs):
    parts, outs = refs[:ADD_PARTS], refs[ADD_PARTS:]
    height = C // ADD_PARTS
    for i, ref in enumerate(parts):
        rows = slice(i * height, (i + 1) * height)
        total = across_ref[rows, :].astype(jnp.float32) + ref[...].astype(jnp.float32)
        first = i * height % outs[0].shape[0]
        out_ref = outs[i * height // outs[0].shape[0]]
        out_ref[first : first + height, :] = total.astype(jnp.bfloat16)


def add_parts(across, parts, pieces):
    return pl.pallas_call(
        add_kernel,
        out_shape=(rows_of(C // pieces, SHARD),) * pieces,
        in_specs=[VMEM] * (1 + len(parts)),
        out_specs=(VMEM,) * pieces,
        compiler_params=kernel_params(8),
        cost_estimate=QUICK,
        name="add",
    )(across, *parts)


def finish_kernel(r, whole, split, plan_ref, *refs):
    held_ref, sems = refs[-2:]
    out_ref = refs[-3]
    slot = plan_ref[2 + r]
    copies = []
    for half in range(2):
        here = slice(half * HALF, (half + 1) * HALF)
        total = sum(ref[here, :].astype(jnp.float32) for ref in refs[:whole])
        for ref in refs[whole : whole + split * (half + 1)][split * half :]:
            total += ref[...].astype(jnp.float32)
        held_ref[here, :] = total.astype(jnp.bfloat16)
        copies += start_all(
            [
                pltpu.make_async_copy(
                    held_ref.at[pl.ds(half * HALF, HALF)],
                    out_ref.at[slot, pl.ds(half * HALF, HALF)],
                    sems.at[half],
                )
            ]
        )
    for copy in copies:
        copy.wait()


def finish(r, plan, addends, halves, hidden):
    earlier = [] if hidden is None else [hidden]
    operands = (plan, *addends, *halves, *earlier)
    return pl.pallas_call(
        functools.partial(finish_kernel, r, len(addends), len(halves) // 2),
        out_shape=rows_of(MAXW, C, SHARD),
        in_specs=[SMEM] + [VMEM] * (len(addends) + len(halves)) + [ANY] * len(earlier),
        out_specs=ANY,
        scratch_shapes=[pltpu.VMEM((C, SHARD), jnp.bfloat16), pltpu.SemaphoreType.DMA((2,))],
        input_output_aliases={len(operands) - 1: 0} if earlier else {},
        compiler_params=kernel_params(8),
        cost_estimate=QUICK,
        name=f"finish_{r}",
    )(*operands)


def pages_kernel(group_ref, counts_ref, destinations_ref, owner_ref, plan_ref, *refs):
    sources, (out_ref, held_ref, filled_ref, sems) = refs[:-4], refs[-4:]
    copies = start_all(
        [
            pltpu.make_async_copy(source, held_ref.at[i], sems.at[i])
            for i, source in enumerate(sources)
        ]
    )
    out_ref[...] = jnp.zeros(out_ref.shape, out_ref.dtype)
    filled_ref[0] = 0
    group = group_ref[0]
    for copy in copies:
        copy.wait()

    def span(s, carry):
        @pl.when(s % (2 * MAXW) < counts_ref[s // (2 * MAXW)])
        def _():
            target = destinations_ref[s]
            holder = target // MAXW
            place = jnp.where(plan_ref[8 + holder] == target % MAXW, 0, 1)
            away = jnp.where(group < holder, group - holder + GROUPS, group - holder)
            for i in range(C // PAGE):
                @pl.when(owner_ref[s * (C // PAGE) + i] == group)
                def _():
                    rank = filled_ref[0]
                    filled_ref[0] = rank + 1
                    out_ref[jnp.minimum(rank, OWNCAP - 1)] = held_ref[
                        away, place, i * PAGE : (i + 1) * PAGE, :
                    ]

        return carry

    lax.fori_loop(0, GROUPS * 2 * MAXW, span, 0)


def place_pages(group, counts, destinations, page_owner, plan, gathered):
    return pl.pallas_call(
        pages_kernel,
        out_shape=rows_of(OWNCAP, PAGE, SLICE),
        in_specs=[SMEM] * 5 + [ANY] * len(gathered),
        out_specs=VMEM,
        scratch_shapes=[
            pltpu.VMEM((GROUPS, 2, C, SLICE), jnp.bfloat16),
            pltpu.SMEM((1,), jnp.int32),
            pltpu.SemaphoreType.DMA((GROUPS,)),
        ],
        cost_estimate=QUICK,
        name="pages",
    )(group, counts, destinations, page_owner, plan, *gathered)


def stay(weight):
    return pltpu.with_memory_space_constraint(weight, pltpu.HBM)


def after(rows, other):
    return lax.optimization_barrier((rows, other))[0]


def routed_layer(
    tokens,
    prefix_kv,
    counts,
    destinations,
    page_owner,
    prefix_len,
    ln_gain,
    q_weight,
    q_bias,
    kv_weight,
    kv_bias,
    o_weight,
):
    group = lax.axis_index("pg").reshape(1)
    column = lax.axis_index("tp")
    columns = column.reshape(1)
    plan, *choices, leave_first, leave_second = route(
        group, counts, destinations, prefix_len, tokens, prefix_kv
    )
    gain = ln_gain.astype(jnp.float32).reshape(KVH, 1, SHARD)
    q_blocks = stay(q_weight.reshape(KVH, SHARD, HEADS * HD))
    kv_blocks = stay(kv_weight.reshape(KVH, SHARD, SLICE))
    o_weight = stay(o_weight)
    q_row, kv_row = q_bias.reshape(1, -1), kv_bias.reshape(1, -1)
    tables = [stay(table) for table in rope_tables()]
    keeps_own = (column == 0) | (column == KVH - 1)

    def swap(rows, step):
        return lax.ppermute(rows, "tp", [(i, i ^ step) for i in range(KVH)])

    def share_head(mine, other):
        passed = swap(other, 1)
        return jnp.where(keeps_own, mine, passed), jnp.where(keeps_own, passed, mine)

    def rotate_groups(rows):
        return [
            lax.ppermute(rows, "pg", [(i, (i + step) % GROUPS) for i in range(GROUPS)])
            for step in range(1, GROUPS)
        ]

    def add_pair(a, b):
        return (a.astype(jnp.float32) + b.astype(jnp.float32)).astype(jnp.bfloat16)

    def first_round(pairs, leaving):
        return lax.ppermute(leaving, "pg", pairs)

    def second_round(pairs, leaving, rows):
        across = swap(rows, 2)
        return lax.ppermute(leaving, "pg", pairs), swap(rows, 1), across, swap(across, 1)

    patterns = round_patterns()
    arrived = lax.switch(
        choices[0][0], [functools.partial(first_round, pairs) for pairs in patterns], leave_first
    )
    rows_0, *old_0 = settle(0, columns, plan, tokens, prefix_kv, arrived)
    leave_second, rows_0 = lax.optimization_barrier((leave_second, rows_0))
    arrived, *others_0 = lax.switch(
        choices[1][0],
        [functools.partial(second_round, pairs) for pairs in patterns],
        leave_second,
        rows_0,
    )
    rows_1, *old_1, top_rows_1, bottom_rows_1 = settle(
        1, columns, plan, tokens, prefix_kv, arrived
    )
    others_0, old_0, rows_1 = lax.optimization_barrier((others_0, old_0, rows_1))

    beside_1 = swap(rows_1, 1)
    top_1 = swap(top_rows_1, 2)
    old_kept_0, old_crossing_0 = share_head(*old_0)
    pieces = [[rows_0]] + [[rows] for rows in others_0]
    normed, fresh_0, *new_0 = fresh_rows(
        0, columns, plan, pieces, gain, kv_blocks, kv_row, tables
    )
    new_kept_0, new_crossing_0 = share_head(*new_0)
    old_crossed_0 = swap(after(old_crossing_0, fresh_0), 2)
    new_crossed_0 = swap(new_crossing_0, 2)
    queries = query_rows(0, plan, after(normed, beside_1), q_blocks, q_row, tables)
    bottom_1 = swap(after(bottom_rows_1, queries), 2)
    old_kept_1, old_crossing_1 = share_head(*old_1)
    old_crossed_1 = swap(after(old_crossing_1, fresh_0), 2)
    _, *corner, beside_0, across, kept_0 = attend(
        0, columns, plan, after(queries, (top_1, old_crossed_1)), (old_kept_0, old_crossed_0),
        (new_kept_0, new_crossed_0), o_weight, (3, 1, 2, 0), ADD_PARTS,
    )
    corner = [swap(rows, 1) for rows in after(corner, bottom_1)]
    sum_top, sum_bottom = add_parts(across, corner, 2)
    total_top = swap(sum_top, 2)
    passed_0 = swap(beside_0, 1)

    pieces = [[after(rows_1, sum_top)], [beside_1], [top_1, bottom_1]]
    pieces.append([swap(rows, 1) for rows in pieces[2]])
    normed, fresh_1, *new_1 = fresh_rows(
        1, columns, plan, pieces, gain, kv_blocks, kv_row, tables
    )
    new_kept_1, new_crossing_1 = share_head(*new_1)
    new_crossed_1 = swap(new_crossing_1, 2)
    queries = query_rows(1, plan, after(normed, passed_0), q_blocks, q_row, tables)
    total_bottom = swap(after(sum_bottom, (queries, new_crossed_1)), 2)
    heads, *corner = attend(
        1, columns, plan, after(queries, total_top), (old_kept_1, old_crossed_1),
        (new_kept_1, new_crossed_1), o_weight, (3,), ADD_PARTS,
    )
    corner = [swap(rows, 1) for rows in corner]
    across, beside_1 = output_blocks(columns, heads, o_weight, (2, 1))
    (sum_all,) = add_parts(across, corner, 1)
    sum_all = after(sum_all, total_bottom)
    total_1 = swap(sum_all, 2)

    fresh = jnp.stack([fresh_0, after(fresh_1, sum_all)])
    gathered = [fresh] + rotate_groups(fresh)
    passed_1 = swap(after(beside_1, sum_all), 1)
    (base_1,) = output_blocks(
        columns, after(heads, sum_all), o_weight, (0,), (rows_1, passed_1), jnp.float32
    )
    hidden = finish(
        0, plan, (rows_0, kept_0, after(passed_0, sum_all)), (total_top, total_bottom), None
    )
    hidden = finish(1, plan, (base_1, total_1), (), hidden)
    kv_pages = place_pages(
        group, counts, destinations, page_owner, plan, after(gathered, hidden)
    )
    return (hidden, kv_pages)


def gathered_layer(
    tokens,
    prefix_kv,
    counts,
    destinations,
    page_owner,
    prefix_len,
    ln_gain,
    q_weight,
    q_bias,
    kv_weight,
    kv_bias,
    o_weight,
):
    groups = lax.axis_size("pg")
    group_index = lax.axis_index("pg")
    column = lax.axis_index("tp")
    source_count = tokens.shape[0]
    heads_here = q_weight.shape[1] // HD
    group_size = HQ // KVH
    local_kv_heads = max(1, heads_here // group_size)
    first_kv_head = column * heads_here // group_size
    slice_width = prefix_kv.shape[2]
    extra_slots = source_count - MAXW
    source, filled, is_valid = work_sources(counts, destinations, groups)
    rank_table = page_ranks(is_valid, page_owner, groups)
    own_sources = lax.dynamic_slice_in_dim(source, group_index * MAXW, MAXW)
    stays_home = jnp.arange(MAXW, dtype=jnp.int32) < counts[group_index]
    spare_index = jnp.arange(groups * extra_slots, dtype=jnp.int32)
    spare_slot = spare_index // extra_slots * source_count + MAXW + spare_index % extra_slots
    spare_valid = MAXW + spare_index % extra_slots < counts[spare_index // extra_slots]
    wanted = group_index * MAXW + jnp.arange(MAXW, dtype=jnp.int32)
    matches = spare_valid[None, :] & (destinations[spare_slot][None, :] == wanted[:, None])
    chosen = jnp.sum(jnp.where(matches, spare_index[None, :], 0), axis=1)

    def settle(own_rows, moved_rows):
        return jnp.where(stays_home[:, None, None], own_rows, moved_rows[chosen])

    gathered = lax.all_gather(prefix_kv, "tp", axis=2, tiled=True)
    head_columns = head_block(gathered, first_kv_head, local_kv_heads)
    moved_tokens, moved_heads = (
        lax.all_gather(tokens[MAXW:], "pg", axis=0, tiled=True),
        lax.all_gather(head_columns[MAXW:], "pg", axis=0, tiled=True),
    )
    work_tokens = settle(tokens[:MAXW], moved_tokens)
    work_prefix = settle(head_columns[:MAXW], moved_heads)
    features = lax.all_gather(work_tokens, "tp", axis=2, tiled=True)
    feature_rows = features.astype(jnp.float32)
    inv_rms = lax.rsqrt(jnp.mean(feature_rows * feature_rows, axis=-1, keepdims=True) + norm_eps)
    normed = (feature_rows * inv_rms * ln_gain.astype(jnp.float32)).astype(jnp.bfloat16)
    flat_normed = normed.reshape(MAXW * C, D)
    queries = jnp.dot(flat_normed, q_weight, preferred_element_type=jnp.float32) + q_bias.astype(
        jnp.float32
    )
    fresh_columns = (
        jnp.dot(flat_normed, kv_weight, preferred_element_type=jnp.float32)
        + kv_bias.astype(jnp.float32)
    ).astype(jnp.bfloat16)
    fresh_all = lax.all_gather(
        fresh_columns.reshape(MAXW, C, slice_width), "tp", axis=2, tiled=True
    )
    prefix_start = prefix_len[own_sources]
    positions = prefix_start[:, None] + jnp.arange(C, dtype=jnp.int32)[None, :]
    cosine, sine_table = rope_angles(positions)
    cosine = cosine[:, :, None, :]
    sine_table = sine_table[:, :, None, :]
    queries = (
        rotate(queries.reshape(MAXW, C, heads_here, HD), cosine, sine_table) * HD ** (-0.5)
    ).astype(jnp.bfloat16)
    fresh_all = fresh_all.reshape(MAXW, C, 2, KVH, HD)
    new_keys = rotate(fresh_all[:, :, 0].astype(jnp.float32), cosine, sine_table).astype(
        jnp.bfloat16
    )
    new_kv = jnp.concatenate(
        [new_keys.reshape(MAXW, C, KVH * HD), fresh_all[:, :, 1].reshape(MAXW, C, KVH * HD)], axis=2
    )
    new_heads = head_block(new_kv, first_kv_head, local_kv_heads)
    all_rows = jnp.concatenate([work_prefix, new_heads], axis=1).reshape(
        MAXW, PRE + C, 2, local_kv_heads, HD
    )
    key_rows = all_rows[:, :, 0]
    value_rows = all_rows[:, :, 1]
    grouped = queries.reshape(MAXW, C, local_kv_heads, heads_here // local_kv_heads, HD)
    scores = jnp.einsum("wcngd,wlnd->wngcl", grouped, key_rows, preferred_element_type=jnp.float32)
    key_index = jnp.arange(PRE + C, dtype=jnp.int32)
    query_row = jnp.arange(C, dtype=jnp.int32)
    allowed = jnp.where(
        key_index[None, None, :] < PRE,
        key_index[None, None, :] < prefix_start[:, None, None],
        (key_index - PRE)[None, None, :] <= query_row[None, :, None],
    )
    scores = jnp.where(allowed[:, None, None], scores, -jnp.inf)
    row_max = jnp.max(scores, axis=-1, keepdims=True)
    weights = jnp.exp(scores - row_max)
    probabilities = (weights / jnp.sum(weights, axis=-1, keepdims=True)).astype(jnp.bfloat16)
    mixed_heads = jnp.einsum(
        "wngcl,wlnd->wcngd", probabilities, value_rows, preferred_element_type=jnp.float32
    ).astype(jnp.bfloat16)
    head_partial = jnp.dot(
        mixed_heads.reshape(MAXW * C, heads_here * HD), o_weight, preferred_element_type=jnp.float32
    ).reshape(MAXW, C, D)
    attended = lax.psum_scatter(
        head_partial.astype(jnp.bfloat16), "tp", scatter_dimension=2, tiled=True
    ).astype(jnp.float32)
    hidden = (work_tokens.astype(jnp.float32) + attended).astype(jnp.bfloat16)
    pages_per = C // PAGE
    own_columns = lax.dynamic_slice_in_dim(new_kv, column * slice_width, slice_width, 2)
    page_rows = own_columns.reshape(MAXW * pages_per, PAGE, slice_width)
    work_page = jnp.arange(groups * MAXW * pages_per, dtype=jnp.int32)
    source_page = source[work_page // pages_per] * pages_per + work_page % pages_per
    owner_of_page = page_owner[source_page]
    local_owner = lax.dynamic_slice_in_dim(
        owner_of_page, group_index * MAXW * pages_per, MAXW * pages_per
    )
    addressed = local_owner[None, :] == jnp.arange(groups, dtype=jnp.int32)[:, None]
    outbox = jnp.where(addressed[:, :, None, None], page_rows[None], jnp.zeros((), jnp.bfloat16))
    arrived = lax.all_to_all(outbox, "pg", split_axis=0, concat_axis=0, tiled=True).reshape(
        groups * MAXW * pages_per, PAGE, slice_width
    )
    retained = filled[work_page // pages_per] & (owner_of_page == group_index)
    slot_matches = retained[None, :] & (
        rank_table[source_page][None, :] == jnp.arange(OWNCAP, dtype=jnp.int32)[:, None]
    )
    slot_pick = jnp.sum(jnp.where(slot_matches, work_page[None, :], 0), axis=1)
    kv_pages = jnp.where(
        jnp.any(slot_matches, axis=1)[:, None, None],
        arrived[slot_pick],
        jnp.zeros((), jnp.bfloat16),
    )
    return (hidden, kv_pages)


def solution(mesh):
    in_specs = (
        P(("parts", "pg"), None, "tp"),
        P(("parts", "pg"), None, "tp"),
        P("parts"),
        P("parts"),
        P("parts"),
        P("parts"),
        P(),
        P(None, "tp"),
        P("tp"),
        P(None, "tp"),
        P("tp"),
        P("tp", None),
    )
    out_specs = (P(("parts", "pg"), None, "tp"), P(("parts", "pg"), None, "tp"))
    if mesh.shape["pg"] == 4 and mesh.shape["tp"] == KVH:
        layer = routed_layer
    else:
        layer = gathered_layer
    return jax.shard_map(layer, mesh=mesh, in_specs=in_specs, out_specs=out_specs, check_vma=False)
```
